512 devices in a mesh: dp: 64 (over z, y), corpus: 8 (over x, core).
Axes of the slice: x: 4, y: 4, z: 16, core: 2. Of those that a mesh axis runs over, the one named last changes fastest.
Arguments:
- queries: bfloat16 [65536, 1024], P(('dp', 'corpus')), may hold values from -6 to 6
- passages: bfloat16 [196608, 1024], P(('dp', 'corpus')), may hold values from -6 to 6
- weight: bfloat16 [1024, 1024], replicated, may hold values from -0.1875 to 0.1875
- pairs: int32 [512, 8], P(('dp', 'corpus')), may hold values from 0 to 23, as said below
- positive: int32 [65536], P(('dp', 'corpus')), may hold values from 0 to 1023
Outputs:
- losses: float32 [65536], P(('dp', 'corpus'))
- query_grad: bfloat16 [65536, 1024], P(('dp', 'corpus'))
- passage_grad: bfloat16 [196608, 1024], P(('dp', 'corpus'))
- weight_grad: float32 [1024, 1024], P('dp')
The draws below stay inside these ranges and needn't reach their ends.
Inputs may be any that keep to these rules, and one draw needn't show every extreme that they name: `pairs`: each row lists 8 distinct blocks of its own data-parallel group; block b of a group sits on corpus shard b // 3 of that group as its block b % 3. No shard holds more than 2 of a row's blocks, and in every row some shard holds exactly 2 of them. `positive`: index into the tile's 8 * 128 candidate passages, in the order of the tile's row of pairs.
All inputs are finite; a program needn't handle non-finite values.
Results may differ from the reference program's by a relative error of at most 0.0057.
Values may be sent and summed in bfloat16 or wider, within the bound.
No kernel may reach another device: no remote copies, remote signals or barrier semaphores. Data moves between devices by JAX's collectives and lax.ppermute only.
A program may use at most 64 MiB of HBM per device.

```python
import jax
import jax.numpy as jnp
from jax import lax

D = 1024
TILE = 128
BDEV = 3
CAP = 2
K = 8
TILES = 512
QTOT = 65536
PTOT = 196608
N_DP = 64
N_CORPUS = 8


def draw_pairs(key, part):
    key = jax.random.fold_in(key, 11)
    key_owner, key_rows = jax.random.split(key)
    owner_order = jax.random.permutation(key_owner, N_CORPUS).astype(jnp.int32)

    def single_row(row_key):
        key_first, key_second, key_own, key_offer, key_rest, key_shuffle = jax.random.split(row_key, 6)
        first = jax.random.randint(key_first, (), 0, N_CORPUS)
        second = jax.random.randint(key_second, (), 0, N_CORPUS)
        favored = owner_order[jnp.minimum(first, second)]
        own_blocks = jax.random.permutation(key_own, BDEV)[:CAP].astype(jnp.int32) + favored * BDEV
        offer_keys = jax.random.split(key_offer, N_CORPUS - 1)
        offered = jax.vmap(lambda offer_key: jax.random.permutation(offer_key, BDEV)[:CAP].astype(jnp.int32))(offer_keys)
        other_owner = jnp.arange(N_CORPUS - 1, dtype=jnp.int32)
        other_owner = other_owner + (other_owner >= favored).astype(jnp.int32)
        offered_blocks = (offered + other_owner[:, None] * BDEV).reshape((N_CORPUS - 1) * CAP)
        rest_pick = jax.random.permutation(key_rest, (N_CORPUS - 1) * CAP)[:K - CAP].astype(jnp.int32)
        rest_blocks = offered_blocks[rest_pick]
        both_lists = jnp.concatenate([own_blocks, rest_blocks])
        return both_lists[jax.random.permutation(key_shuffle, K)]
    row_keys = jax.random.split(key_rows, TILES)
    return jax.vmap(single_row)(row_keys).astype(jnp.int32)


def set_ends(result, rng, least, top_value):
    index_at = [jax.random.randint(jax.random.fold_in(rng, axis), (), 0, length) for axis, length in enumerate(result.shape)]
    longest = result.shape.index(max(result.shape))
    next_to = index_at[:longest] + [(index_at[longest] + 1) % result.shape[longest]] + index_at[longest + 1:]
    return result.at[tuple(index_at)].set(least).at[tuple(next_to)].set(top_value)


def levels(stream_key, shape, cuts, smallest, high):
    factor_of = 1.0
    for dim, blocks in cuts:
        steps = jax.random.uniform(jax.random.fold_in(jax.random.fold_in(stream_key, 6), dim), (blocks,), jnp.float32, smallest / len(cuts), high / len(cuts))
        factor_of = factor_of * jnp.repeat(jnp.exp(steps), shape[dim] // blocks).reshape((-1,) + (1,) * (len(shape) - 1 - dim))
    return factor_of


def scatter_about(stream_key, extent, deviation, reach, pieces=(), held_as=jnp.bfloat16):
    entries = deviation * jax.random.normal(stream_key, extent, jnp.float32)
    if pieces:
        entries = entries * levels(stream_key, extent, pieces, -0.22, 0.18)
    return jnp.clip(entries, -reach, reach).astype(held_as)


def setup_inputs(seed: int = 0) -> dict:
    streams_of = jax.random.split(jax.random.key(seed), 6)
    queries = scatter_about(streams_of[0], (QTOT, D), 1.0, 6.0, ((0, 512),))
    passages = scatter_about(streams_of[1], (PTOT, D), 1.0, 6.0, ((0, 512),))
    weight = scatter_about(streams_of[2], (D, D), D ** -0.5, 0.1875)
    pairs = draw_pairs(jax.random.fold_in(streams_of[5], 71), 0)
    positive = set_ends(jax.random.randint(streams_of[4], (QTOT,), 0, K * TILE), jax.random.fold_in(streams_of[4], 1), 0, (K * TILE) - 1).astype(jnp.int32)
    return {"queries": queries, "passages": passages, "weight": weight, "pairs": pairs, "positive": positive}


score_scale = 50.0
epsilon = 1e-06

def normalize(proj):
    return proj * lax.rsqrt(lax.optimization_barrier(jnp.sum(proj * proj, axis=-1, keepdims=True)) + epsilon)

def tile_terms(query_tile, candidates, positive_tile):
    scores = lax.dot_general(query_tile, candidates, (((1,), (1,)), ((), ())), preferred_element_type=jnp.float32) * score_scale
    exponent = jnp.exp(scores)
    exp_total = lax.optimization_barrier(jnp.sum(exponent, axis=1))
    picked = jnp.take_along_axis(scores, positive_tile[:, None], axis=1)[:, 0]
    losses = jnp.log(exp_total) - picked
    column = jnp.arange(candidates.shape[0], dtype=jnp.int32)
    target = (column[None, :] == positive_tile[:, None]).astype(jnp.float32)
    dscore = (exponent / exp_total[:, None] - target).astype(jnp.bfloat16)
    query_grad = jnp.dot(dscore, candidates, preferred_element_type=jnp.float32) * score_scale
    block_term = lax.dot_general(dscore, query_tile, (((0,), (0,)), ((), ())), preferred_element_type=jnp.float32) * score_scale
    return (losses, query_grad, block_term.astype(jnp.bfloat16))

def project_back(proj_back, weight):
    return lax.dot_general(proj_back, weight, (((1,), (1,)), ((), ())), preferred_element_type=jnp.float32).astype(jnp.bfloat16)

def reference(queries, passages, weight, pairs, positive):
    query_groups = queries.reshape(N_DP, N_CORPUS * TILE, D)
    passage_groups = passages.reshape(N_DP, N_CORPUS * BDEV * TILE, D)
    pair_groups = pairs.reshape(N_DP, N_CORPUS, K)
    positive_groups = positive.reshape(N_DP, N_CORPUS, TILE)

    def group_step(weight_total, group_slices):
        query_rows, passage_rows, named_blocks, positive_rows = group_slices
        query_proj = jnp.dot(query_rows, weight, preferred_element_type=jnp.float32)
        passage_proj = jnp.dot(passage_rows, weight, preferred_element_type=jnp.float32)
        query_emb = normalize(query_proj).astype(jnp.bfloat16)
        passage_emb = normalize(passage_proj).astype(jnp.bfloat16)
        blocks = passage_emb.reshape(N_CORPUS * BDEV, TILE, D)

        def per_tile(tile_args):
            query_tile, tile_pairs, positive_tile = tile_args
            candidates = blocks[tile_pairs].reshape(K * TILE, D)
            return tile_terms(query_tile, candidates, positive_tile)
        losses, query_grad, block_term = lax.map(per_tile, (query_emb.reshape(N_CORPUS, TILE, D), named_blocks, positive_rows))
        passage_grad = jnp.zeros((N_CORPUS * BDEV, TILE, D), jnp.float32)
        passage_grad = passage_grad.at[named_blocks.reshape(N_CORPUS * K)].add(block_term.reshape(N_CORPUS * K, TILE, D).astype(jnp.float32))
        query_back = jax.vjp(normalize, query_proj)[1](query_grad.reshape(N_CORPUS * TILE, D))[0].astype(jnp.bfloat16)
        passage_back = jax.vjp(normalize, passage_proj)[1](passage_grad.reshape(N_CORPUS * BDEV * TILE, D))[0].astype(jnp.bfloat16)
        query_hidden = project_back(query_back, weight)
        passage_hidden = project_back(passage_back, weight)
        weight_term = lax.dot_general(query_rows, query_back, (((0,), (0,)), ((), ())), preferred_element_type=jnp.float32)
        weight_term = weight_term + lax.dot_general(passage_rows, passage_back, (((0,), (0,)), ((), ())), preferred_element_type=jnp.float32)
        return (weight_total + weight_term, (losses.reshape(N_CORPUS * TILE), query_hidden, passage_hidden))
    weight_total, outputs = lax.scan(group_step, jnp.zeros((D, D), jnp.float32), (query_groups, passage_groups, pair_groups, positive_groups))
    losses, query_hidden, passage_hidden = outputs
    return (losses.reshape(QTOT), query_hidden.reshape(QTOT, D), passage_hidden.reshape(PTOT, D), weight_total / TILES)
```

```python
import jax
import jax.numpy as jnp
from jax import lax
from jax.sharding import Mesh, PartitionSpec as P

score_scale = 50.0
epsilon = 1e-06

X, C, Y, Z = 4, 2, 4, 16
SWAP = ((0, 1), (1, 0))


def exchange(value, axis):
    return lax.all_to_all(value, axis, split_axis=0, concat_axis=0, tiled=True)


def gather(value, axis, size):
    return exchange(jnp.broadcast_to(value[None], (size,) + value.shape), axis)


def matmul(a, b):
    return jnp.dot(a, b, preferred_element_type=jnp.float32)


def matmul_tn(a, b):
    return lax.dot_general(a, b, (((0,), (0,)), ((), ())), preferred_element_type=jnp.float32)


def matmul_nt(a, b):
    return lax.dot_general(a, b, (((1,), (1,)), ((), ())), preferred_element_type=jnp.float32)


def inverse_norm(proj):
    return lax.rsqrt(jnp.sum(proj * proj, axis=-1, keepdims=True) + epsilon)


def back_of(proj, r, grad):
    inner = jnp.sum(proj * grad, axis=-1, keepdims=True)
    return (r * grad - (r * r * r * inner) * proj).astype(jnp.bfloat16)


def body(queries, passages, weight, pairs, positive):
    rows, width = queries.shape
    own_p = passages.shape[0]
    blocks = own_p // rows
    chip_blocks = blocks * C
    names = pairs.shape[1]
    x = lax.axis_index("x")
    c = lax.axis_index("c")

    tiles = gather(queries, "x", X)
    index = jnp.concatenate([positive, pairs[0], jnp.zeros((rows - names,), jnp.int32)])
    index = gather(index.reshape(2, rows), "x", X)
    sibling = lax.ppermute(passages, "c", SWAP)

    chip_passages = jnp.concatenate([passages, sibling], axis=0)
    p_proj = matmul(chip_passages, weight)
    p_r = inverse_norm(p_proj)
    p_emb = (p_proj * p_r).astype(jnp.bfloat16)

    tile_positive = index[:, 0]
    tile_pairs = index[:, 1, :names]
    local = tile_pairs - x * chip_blocks
    slot = jnp.where((local >= 0) & (local < chip_blocks), (local + blocks * c) % chip_blocks, -1)
    named = jnp.any(slot[:, :, None] == jnp.arange(chip_blocks)[None, None, :], axis=1)
    pos_name = tile_positive // rows
    pos_slot = jnp.sum(
        jnp.where(pos_name[:, :, None] == jnp.arange(names)[None, None, :], slot[:, None, :], 0), axis=2
    )
    pos_column = jnp.where(pos_slot >= 0, pos_slot * rows + tile_positive % rows, -1).reshape(-1, 1)
    column = jnp.arange(chip_blocks * rows, dtype=jnp.int32)[None, :]
    target = column == pos_column
    mask = jnp.repeat(jnp.repeat(named, rows, axis=1), rows, axis=0)

    chip_queries = tiles.reshape(X * rows, width)
    q_proj = matmul(chip_queries, weight)
    q_r = inverse_norm(q_proj)
    q_emb = (q_proj * q_r).astype(jnp.bfloat16)
    scores = matmul_nt(q_emb, p_emb) * score_scale
    exponent = jnp.where(mask, jnp.exp(scores), 0.0)
    part_total = jnp.sum(exponent, axis=1)
    part_picked = jnp.sum(jnp.where(target, scores, 0.0), axis=1)
    outgoing = jnp.concatenate(
        [
            jnp.broadcast_to(part_total.reshape(1, X, rows), (X, X, rows)),
            part_picked.reshape(X, 1, rows),
        ],
        axis=1,
    )
    sums = jnp.sum(exchange(outgoing, "x"), axis=0)
    total = sums[:X]
    own_total = jnp.sum(jnp.where((jnp.arange(X) == x)[:, None], total, 0.0), axis=0)
    losses = jnp.log(own_total) - sums[X]
    dscore = (exponent / total.reshape(-1, 1) - target.astype(jnp.float32)).astype(jnp.bfloat16)

    q_grad = matmul(dscore, p_emb) * score_scale
    p_grad = matmul_tn(dscore, q_emb) * score_scale
    q_back = back_of(q_proj, q_r, q_grad)
    p_back = back_of(p_proj, p_r, p_grad)

    half = width // C
    backs = jnp.concatenate([q_back, p_back], axis=0)
    hidden = jnp.concatenate([chip_queries, chip_passages], axis=0)
    backs_there = lax.dynamic_slice_in_dim(backs, (1 - c) * half, half, axis=1)
    backs_here = lax.dynamic_slice_in_dim(backs, c * half, half, axis=1)
    w_there = lax.ppermute(matmul_tn(hidden, backs_there).astype(jnp.bfloat16), "c", SWAP)
    w_here = matmul_tn(hidden, backs_here) + w_there.astype(jnp.float32)
    own_rows = width // (Z * Y)
    w = w_here.astype(jnp.bfloat16).reshape(Z, Y, own_rows, half).transpose(1, 0, 2, 3)
    w = jnp.sum(exchange(w, "y").astype(jnp.float32), axis=0)
    w = w.astype(jnp.bfloat16).reshape(Z, own_rows, X, half // X).transpose(2, 0, 1, 3)
    w = jnp.sum(exchange(w, "x").astype(jnp.float32), axis=0)
    w = jnp.sum(exchange(w.astype(jnp.bfloat16), "z").astype(jnp.float32), axis=0)
    w = gather(w * (1.0 / (Z * Y * X * C)), ("x", "c"), X * C)
    weight_grad = w.reshape(X, C, own_rows, half // X).transpose(2, 1, 0, 3).reshape(own_rows, width)

    q_sum = jnp.sum(
        exchange(q_grad.astype(jnp.bfloat16).reshape(X, rows, width), "x").astype(jnp.float32), axis=0
    )
    own_proj = lax.dynamic_slice_in_dim(q_proj, x * rows, rows, axis=0)
    own_r = lax.dynamic_slice_in_dim(q_r, x * rows, rows, axis=0)
    query_grad = matmul_nt(back_of(own_proj, own_r, q_sum), weight).astype(jnp.bfloat16)

    p_sum = p_grad[:own_p] + lax.ppermute(p_grad[own_p:].astype(jnp.bfloat16), "c", SWAP).astype(jnp.float32)
    passage_grad = matmul_nt(back_of(p_proj[:own_p], p_r[:own_p], p_sum), weight).astype(jnp.bfloat16)
    return losses, query_grad, passage_grad, weight_grad


def solution(mesh):
    torus = Mesh(mesh.devices.reshape(Z, Y, X, C), ("z", "y", "x", "c"))
    every = ("z", "y", "x", "c")
    return jax.shard_map(
        body,
        mesh=torus,
        in_specs=(P(every, None), P(every, None), P(), P(every, None), P(every)),
        out_specs=(P(every), P(every, None), P(every, None), P(("z", "y"), None)),
        check_vma=False,
    )
```

```python
import jax
import jax.numpy as jnp
from jax import lax
from jax.experimental import pallas as pl
from jax.experimental.pallas import tpu as pltpu
from jax.sharding import Mesh, PartitionSpec as P

score_scale = 50.0
epsilon = 1e-06

X, C, Y, Z = 4, 2, 4, 16
SWAP = ((0, 1), (1, 0))
ROWS = 128
WIDTH = 1024
OWN = 384
BLOCKS = OWN // ROWS
CHIP_BLOCKS = BLOCKS * C
NAMES = 8
EXTRA = 16
HALF = WIDTH // C
PART = 256
HBM = pl.BlockSpec(memory_space=pltpu.HBM)
VMEM = pl.BlockSpec(memory_space=pltpu.VMEM)
SMEM = pl.BlockSpec(memory_space=pltpu.SMEM)
F32, BF16 = jnp.float32, jnp.bfloat16


def shift(k):
    return tuple(((i + k) % X, i) for i in range(X))


def exchange(value, axis):
    return lax.all_to_all(value, axis, split_axis=0, concat_axis=0, tiled=True)


def matmul(a, b):
    return jnp.dot(a, b, preferred_element_type=F32)


def matmul_tn(a, b):
    return lax.dot_general(a, b, (((0,), (0,)), ((), ())), preferred_element_type=F32)


def matmul_nt(a, b):
    return lax.dot_general(a, b, (((1,), (1,)), ((), ())), preferred_element_type=F32)


def back_of(emb, r, grad):
    emb = emb.astype(F32)
    inner = jnp.sum(emb * grad, axis=-1, keepdims=True)
    return r * (grad - inner * emb)


def params(mib):
    return pltpu.CompilerParams(vmem_limit_bytes=mib << 20)


def shape(dims, dtype):
    return jax.ShapeDtypeStruct(dims, dtype)


def call(kernel, name, out_shape, in_specs, out_specs, scratch, mib, flops, moved, *args):
    return pl.pallas_call(
        kernel,
        name=name,
        out_shape=out_shape,
        in_specs=in_specs,
        out_specs=out_specs,
        scratch_shapes=scratch,
        compiler_params=params(mib),
        cost_estimate=pl.CostEstimate(flops=flops, bytes_accessed=moved, transcendentals=0),
    )(*args)


def pack_kernel(queries, positive, pairs, out, pos, names, wide, narrow, sems):
    copies = [pltpu.make_async_copy(positive, pos, sems.at[0]), pltpu.make_async_copy(pairs, names, sems.at[1])]
    for d in range(X):
        copies.append(pltpu.make_async_copy(queries, out.at[d, pl.ds(0, ROWS)], sems.at[2 + d]))
    for copy in copies:
        copy.start()
    wide[...] = jnp.full(wide.shape, 255.0, F32)
    copies[0].wait()
    copies[1].wait()
    index = pos[...]
    wide[0:1, 0:ROWS] = (index >> 7).astype(F32)
    wide[0:1, ROWS : 2 * ROWS] = (index & 127).astype(F32)
    wide[0:1, 2 * ROWS : 2 * ROWS + NAMES] = names[...].astype(F32)
    narrow[...] = wide[...].astype(BF16)
    for d in range(X):
        copies.append(pltpu.make_async_copy(narrow, out.at[d, pl.ds(ROWS, EXTRA)], sems.at[2 + X + d]))
        copies[-1].start()
    for copy in copies[2:]:
        copy.wait()


def pack(queries, positive, pairs):
    return call(
        pack_kernel, "pack",
        shape((X, ROWS + EXTRA, WIDTH), BF16),
        [HBM, HBM, HBM],
        HBM,
        [
            pltpu.VMEM((1, ROWS), jnp.int32),
            pltpu.VMEM((1, NAMES), jnp.int32),
            pltpu.VMEM((EXTRA, WIDTH), F32),
            pltpu.VMEM((EXTRA, WIDTH), BF16),
            pltpu.SemaphoreType.DMA((2 + 2 * X,)),
        ],
        4, 0, 1_400_000,
        queries, positive.reshape(1, ROWS), pairs,
    )


def project(source, weight, proj, r_out, emb, rows):
    for j in range(WIDTH // PART):
        cols = pl.ds(j * PART, PART)
        proj[:, cols] = matmul(source, weight[:, cols])
    for i in range(rows // ROWS):
        here = pl.ds(i * ROWS, ROWS)
        value = proj[here, :]
        r = lax.rsqrt(jnp.sum(value * value, axis=1, keepdims=True) + epsilon)
        r_out[here, :] = r
        emb[here, :] = (value * r).astype(BF16)


def passage_kernel(passages, weight, emb, r_out, proj):
    project(passages[...], weight, proj, r_out, emb, OWN)


def passage_side(passages, weight):
    return call(
        passage_kernel, "passage_side",
        (shape((OWN, WIDTH), BF16), shape((OWN, 1), F32)),
        [VMEM, VMEM],
        (VMEM, VMEM),
        [pltpu.VMEM((OWN, WIDTH), F32)],
        16, 2 * OWN * WIDTH * WIDTH, 4_000_000,
        passages, weight,
    )


def flat(value):
    return jnp.concatenate([value[k : k + 1] for k in range(X)], axis=1)


def rows_of(tiles, cols=slice(None)):
    return [tiles[k, 0:ROWS, cols] for k in range(X)]


def score_kernel(place, tiles, weight, emb_own, emb_sib, q_emb, q_r, exponent, send, pos_row, proj):
    x, c = place[0], place[1]
    lines = [tiles[k, ROWS : ROWS + EXTRA, 0 : 3 * ROWS].astype(F32)[0:1] for k in range(X)]
    lines = jnp.concatenate(lines, axis=0).astype(jnp.int32)
    pos_name, pos_rest = lines[:, :ROWS], lines[:, ROWS : 2 * ROWS]
    local = lines[:, 2 * ROWS : 3 * ROWS] - x * CHIP_BLOCKS
    turned = local + BLOCKS * c
    turned = jnp.where(turned >= CHIP_BLOCKS, turned - CHIP_BLOCKS, turned)
    slot = jnp.where((local >= 0) & (local < CHIP_BLOCKS), turned, -1)
    lane = lax.broadcasted_iota(jnp.int32, (X, ROWS), 1)
    pos_slot = jnp.full((X, ROWS), -1, jnp.int32)
    for n in range(NAMES):
        of_name = jnp.max(jnp.where(lane == n, slot, -1), axis=1, keepdims=True)
        pos_slot = jnp.where(pos_name == n, of_name, pos_slot)
    pos = flat(jnp.where(pos_slot >= 0, pos_slot * ROWS + pos_rest, -1))
    pos_row[...] = pos

    project(jnp.concatenate(rows_of(tiles), axis=0), weight, proj, q_r, q_emb, X * ROWS)
    line = lax.broadcasted_iota(jnp.int32, (ROWS, X * ROWS), 0)
    total = jnp.zeros((1, X * ROWS), F32)
    picked = jnp.zeros((1, X * ROWS), F32)
    for b in range(CHIP_BLOCKS):
        block = pl.ds(b * ROWS, ROWS)
        named = jnp.max(jnp.where(slot == b, 1, 0), axis=1, keepdims=True)
        named = flat(jnp.broadcast_to(named, (X, ROWS)))
        emb = (emb_own if b < BLOCKS else emb_sib)[pl.ds(b % BLOCKS * ROWS, ROWS), :]
        scores = matmul_nt(emb, q_emb[...]) * score_scale
        value = jnp.where(named > 0, jnp.exp(scores), 0.0)
        exponent[block, :] = value
        total = total + jnp.sum(value, axis=0, keepdims=True)
        picked = picked + jnp.sum(jnp.where(line == pos - b * ROWS, scores, 0.0), axis=0, keepdims=True)
    send[...] = jnp.zeros(send.shape, F32)
    for k in range(X):
        lanes = slice(k * ROWS, (k + 1) * ROWS)
        for d in range(X):
            send[d, k : k + 1, :] = total[:, lanes]
        send[k, X : X + 1, :] = picked[:, lanes]


def score_side(place, tiles, weight, emb_own, emb_sib):
    queries = X * ROWS
    passages = CHIP_BLOCKS * ROWS
    return call(
        score_kernel, "score_side",
        (
            shape((queries, WIDTH), BF16),
            shape((queries, 1), F32),
            shape((passages, queries), F32),
            shape((X, 8, ROWS), F32),
            shape((1, queries), jnp.int32),
        ),
        [SMEM] + [VMEM] * 4,
        (VMEM,) * 5,
        [pltpu.VMEM((queries, WIDTH), F32)],
        24, 2_000_000_000, 8_000_000,
        place, tiles, weight, emb_own, emb_sib,
    )


def grad_kernel(
    place, recv, pos_row, q_r, r_own, r_sib, exponent, q_emb, emb_own, emb_sib, tiles, own, sib,
    losses, g0, g1, g2, g3, emb_mine, r_mine, p_grad_own, p_grad_sib, backs_here, w_there,
    dscore, q_grad, backs,
):
    x, c = place[0], place[1]
    queries = X * ROWS
    total = recv[0] + recv[1] + recv[2] + recv[3]
    mine = jnp.zeros((1, ROWS), F32)
    for k in range(X):
        mine = mine + jnp.where(x == k, total[k : k + 1], 0.0)
    losses[...] = jnp.log(mine) - total[X : X + 1]
    inverse = 1.0 / flat(total)
    pos = pos_row[...]
    line = lax.broadcasted_iota(jnp.int32, (ROWS, queries), 0)
    for b in range(CHIP_BLOCKS):
        block = pl.ds(b * ROWS, ROWS)
        target = jnp.where(line == pos - b * ROWS, 1.0, 0.0)
        dscore[block, :] = (exponent[block, :] * inverse - target).astype(BF16)

    def keep(rows, emb, r, grad):
        value = back_of(emb, r, grad).astype(BF16)
        for h in range(C):
            backs[h, rows, :] = value[:, h * HALF : (h + 1) * HALF]

    for j in range(WIDTH // PART):
        cols = pl.ds(j * PART, PART)
        emb = jnp.concatenate([emb_own[:, cols], emb_sib[:, cols]], axis=0)
        q_grad[:, cols] = matmul_tn(dscore[...], emb) * score_scale
    for k in range(X):
        rows = pl.ds(k * ROWS, ROWS)
        keep(rows, q_emb[rows, :], q_r[rows, :], q_grad[rows, :])
    for k, out in enumerate((g0, g1, g2, g3)):
        rows = pl.ds(pl.multiple_of(lax.rem(x + k, X) * ROWS, ROWS), ROWS)
        out[...] = q_grad[rows, :].astype(out.dtype)
    rows = pl.ds(pl.multiple_of(x * ROWS, ROWS), ROWS)
    emb_mine[...] = q_emb[rows, :]
    r_mine[...] = q_r[rows, :]
    for b in range(CHIP_BLOCKS):
        rows = pl.ds(b * ROWS, ROWS)
        grad = matmul(dscore[rows, :], q_emb[...]) * score_scale
        first = b < BLOCKS
        near = pl.ds((b % BLOCKS) * ROWS, ROWS)
        (p_grad_own if first else p_grad_sib)[near, :] = grad.astype(F32 if first else BF16)
        emb = (emb_own if first else emb_sib)[near, :]
        r = (r_own if first else r_sib)[near, :]
        keep(pl.ds(queries + b * ROWS, ROWS), emb, r, grad)
    weight_terms(tiles, own, sib, backs.at[1 - c], w_there)
    backs_here[...] = backs[c]


def weight_terms(tiles, own, sib, backs, out):
    for j in range(WIDTH // PART):
        cols = pl.ds(j * PART, PART)
        hidden = jnp.concatenate(rows_of(tiles, cols) + [own[:, cols], sib[:, cols]], axis=0)
        out[cols, :] = matmul_tn(hidden, backs[...]).astype(out.dtype)


def grad_side(*args):
    queries = X * ROWS
    passages = CHIP_BLOCKS * ROWS
    tile = shape((ROWS, WIDTH), BF16)
    return call(
        grad_kernel, "grad_side",
        (
            shape((1, ROWS), F32),
            shape((ROWS, WIDTH), F32), tile, tile, tile,
            tile,
            shape((ROWS, 1), F32),
            shape((OWN, WIDTH), F32),
            shape((OWN, WIDTH), BF16),
            shape((queries + passages, HALF), BF16),
            shape((WIDTH, HALF), BF16),
        ),
        [SMEM] + [VMEM] * 12,
        (VMEM,) * 11,
        [
            pltpu.VMEM((passages, queries), BF16),
            pltpu.VMEM((queries, WIDTH), F32),
            pltpu.VMEM((C, queries + passages, HALF), BF16),
        ],
        32, 3_000_000_000, 14_000_000,
        *args,
    )


def weight_kernel(backs, tiles, own, sib, out):
    weight_terms(tiles, own, sib, backs, out)


def weight_here(backs, tiles, own, sib):
    return call(
        weight_kernel, "weight_here",
        shape((WIDTH, HALF), F32),
        [VMEM] * 4,
        VMEM,
        [],
        24, 1_350_000_000, 6_000_000,
        backs, tiles, own, sib,
    )


def spread_kernel(here, there, out):
    own_rows = WIDTH // (Z * Y)
    lanes = HALF // X
    for z in range(Z):
        rows = pl.ds(z * Y * own_rows, Y * own_rows)
        value = (here[rows, :] + there[rows, :].astype(F32)).astype(BF16)
        for y in range(Y):
            for x in range(X):
                out[y * X + x, z] = value[y * own_rows : (y + 1) * own_rows, x * lanes : (x + 1) * lanes]


def spread(here, there):
    return call(
        spread_kernel, "spread",
        shape((Y * X, Z, WIDTH // (Z * Y), HALF // X), BF16),
        [VMEM, VMEM],
        VMEM,
        [],
        16, 500_000, 4_000_000,
        here, there,
    )


def sum_kernel(pieces, out):
    total = pieces[0].astype(F32)
    for k in range(1, Y * X):
        total = total + pieces[k].astype(F32)
    out[...] = total.astype(BF16)


def sum_pieces(pieces):
    return call(
        sum_kernel, "sum_pieces", shape(pieces.shape[1:], BF16), [VMEM], VMEM, [], 8, 500_000, 1_000_000, pieces
    )


def last_sum_kernel(pieces, out):
    total = pieces[0].astype(F32)
    for k in range(1, Z):
        total = total + pieces[k].astype(F32)
    total = total * (1.0 / (Z * Y * X * C))
    for d in range(X * C):
        out[d] = total


def last_sum(pieces):
    dims = (X * C,) + pieces.shape[1:]
    return call(
        last_sum_kernel, "last_sum", shape(dims, F32), [VMEM], VMEM, [], 8, 50_000, 100_000, pieces
    )


def lay_kernel(pieces, out):
    lanes = HALF // X
    for x in range(X):
        for c in range(C):
            out[:, c * HALF + x * lanes : c * HALF + (x + 1) * lanes] = pieces[x * C + c]


def lay(pieces):
    dims = (WIDTH // (Z * Y), WIDTH)
    return call(lay_kernel, "lay", shape(dims, F32), [VMEM], VMEM, [], 8, 0, 200_000, pieces)


def hidden_kernel(*refs):
    *terms, emb, r, weight, out = refs
    grad = terms[0][...]
    for term in terms[1:]:
        grad = grad + term[...].astype(F32)
    back = back_of(emb[...], r[...], grad).astype(BF16)
    for j in range(WIDTH // PART):
        cols = pl.ds(j * PART, PART)
        out[:, cols] = matmul_nt(back, weight[cols, :]).astype(BF16)


def hidden_grad(terms, emb, r, weight):
    rows = emb.shape[0]
    return call(
        hidden_kernel, "hidden_grad",
        shape((rows, WIDTH), BF16),
        [VMEM] * (len(terms) + 3),
        VMEM,
        [],
        24, 2 * rows * WIDTH * WIDTH, 2_000_000 + rows * 10_000,
        *terms, emb, r, weight,
    )


def body(queries, passages, weight, pairs, positive):
    x = lax.axis_index("x")
    c = lax.axis_index("c")
    place = jnp.stack([x, c]).astype(jnp.int32)

    packed = pack(queries, positive, pairs)
    tiles = exchange(packed, "x")
    passages, weight, _ = lax.optimization_barrier((passages, weight, packed))
    emb_own, r_own = passage_side(passages, weight)
    outgoing, _ = lax.optimization_barrier((passages, emb_own))
    sibling = lax.ppermute(outgoing, "c", SWAP)
    emb_sib, r_sib = passage_side(sibling, weight)

    q_emb, q_r, exponent, send, pos_row = score_side(place, tiles, weight, emb_own, emb_sib)
    recv = exchange(send, "x")
    losses, g0, g1, g2, g3, emb_mine, r_mine, p_grad, p_grad_sib, backs, w_there = grad_side(
        place, recv, pos_row, q_r, r_own, r_sib, exponent, q_emb, emb_own, emb_sib, tiles, passages, sibling
    )

    w_there = lax.ppermute(w_there, "c", SWAP)
    w = spread(weight_here(backs, tiles, passages, sibling), w_there)
    p_grad_sib, _ = lax.optimization_barrier((p_grad_sib, w_there))
    p_grad_sib = lax.ppermute(p_grad_sib, "c", SWAP)
    passage_grad = hidden_grad((p_grad, p_grad_sib), emb_own, r_own, weight)

    w = sum_pieces(exchange(w, ("y", "x")))
    w, passage_grad = lax.optimization_barrier((w, passage_grad))
    (g1, g2, g3), w = lax.optimization_barrier(((g1, g2, g3), w))
    terms = [g0] + [lax.ppermute(term, "x", shift(X - k)) for k, term in enumerate((g1, g2, g3), 1)]
    query_grad = hidden_grad(terms, emb_mine, r_mine, weight)

    w = last_sum(exchange(w, "z"))
    weight_grad = lay(exchange(w, ("x", "c")))
    return losses.reshape(ROWS), query_grad, passage_grad, weight_grad


def solution(mesh):
    torus = Mesh(mesh.devices.reshape(Z, Y, X, C), ("z", "y", "x", "c"))
    every = ("z", "y", "x", "c")
    return jax.shard_map(
        body,
        mesh=torus,
        in_specs=(P(every, None), P(every, None), P(), P(every, None), P(every)),
        out_specs=(P(every), P(every, None), P(every, None), P(("z", "y"), None)),
        check_vma=False,
    )
```

```python
import jax
import jax.numpy as jnp
from jax import lax
from jax.experimental import pallas as pl
from jax.experimental.pallas import tpu as pltpu
from jax.sharding import Mesh, PartitionSpec as P

score_scale = 50.0
epsilon = 1e-06

X, C, Y, Z = 4, 2, 4, 16
SWAP = ((0, 1), (1, 0))
ROWS = 128
WIDTH = 1024
OWN = 384
BLOCKS = OWN // ROWS
CHIP_BLOCKS = BLOCKS * C
NAMES = 8
LANES = 128
PIECES = WIDTH // LANES
EXTRA = 16
LINES = PIECES * ROWS + EXTRA
HALF = WIDTH // C
PART = 256
HBM = pl.BlockSpec(memory_space=pltpu.HBM)
VMEM = pl.BlockSpec(memory_space=pltpu.VMEM)
SMEM = pl.BlockSpec(memory_space=pltpu.SMEM)
F32, BF16 = jnp.float32, jnp.bfloat16
SCORE = 24
GRAD = 32


def shift(k):
    return tuple(((i + k) % X, i) for i in range(X))


def exchange(value, axis):
    return lax.all_to_all(value, axis, split_axis=0, concat_axis=0, tiled=True)


def matmul(a, b):
    return jnp.dot(a, b, preferred_element_type=F32)


def matmul_tn(a, b):
    return lax.dot_general(a, b, (((0,), (0,)), ((), ())), preferred_element_type=F32)


def matmul_nt(a, b):
    return lax.dot_general(a, b, (((1,), (1,)), ((), ())), preferred_element_type=F32)


def back_of(emb, r, grad):
    emb = emb.astype(F32)
    inner = jnp.sum(emb * grad, axis=-1, keepdims=True)
    return r * (grad - inner * emb)


def params(mib):
    return pltpu.CompilerParams(vmem_limit_bytes=mib << 20)


def in_hbm(*values):
    return [pltpu.with_memory_space_constraint(value, pltpu.HBM) for value in values]


def shape(dims, dtype):
    return jax.ShapeDtypeStruct(dims, dtype)


def call(kernel, name, out_shape, in_specs, out_specs, scratch, mib, flops, moved, *args):
    return pl.pallas_call(
        kernel,
        name=name,
        out_shape=out_shape,
        in_specs=in_specs,
        out_specs=out_specs,
        scratch_shapes=scratch,
        compiler_params=params(mib),
        cost_estimate=pl.CostEstimate(flops=flops, bytes_accessed=moved, transcendentals=0),
    )(*args)


def pack_kernel(queries, positive, pairs, out, pos, names, rows, wide, packed, sems):
    inner = [
        pltpu.make_async_copy(queries, rows, sems.at[X]),
        pltpu.make_async_copy(positive, pos, sems.at[X + 1]),
        pltpu.make_async_copy(pairs, names, sems.at[X + 2]),
    ]
    for copy in inner:
        copy.start()
    wide[...] = jnp.full(wide.shape, 255.0, F32)
    inner[1].wait()
    inner[2].wait()
    index = pos[...]
    wide[0:1, :] = (index >> 7).astype(F32)
    wide[1:2, :] = (index & 127).astype(F32)
    wide[2:3, 0:NAMES] = names[...].astype(F32)
    packed[pl.ds(PIECES * ROWS, EXTRA), :] = wide[...].astype(BF16)
    inner[0].wait()
    for j in range(PIECES):
        packed[pl.ds(j * ROWS, ROWS), :] = rows[:, j * LANES : (j + 1) * LANES]
    copies = [pltpu.make_async_copy(packed, out.at[d], sems.at[d]) for d in range(X)]
    for copy in copies:
        copy.start()
    for copy in copies:
        copy.wait()


def pack(queries, positive, pairs):
    return call(
        pack_kernel, "pack",
        pltpu.HBM((X, LINES, LANES), BF16),
        [HBM, HBM, HBM],
        HBM,
        [
            pltpu.VMEM((1, ROWS), jnp.int32),
            pltpu.VMEM((1, NAMES), jnp.int32),
            pltpu.VMEM((ROWS, WIDTH), BF16),
            pltpu.VMEM((EXTRA, LANES), F32),
            pltpu.VMEM((LINES, LANES), BF16),
            pltpu.SemaphoreType.DMA((X + 3,)),
        ],
        4, 0, 1_400_000,
        *in_hbm(queries, positive.reshape(1, ROWS), pairs),
    )


def project(source, weight, proj, r_out, emb, rows):
    for j in range(WIDTH // PART):
        cols = pl.ds(j * PART, PART)
        proj[:, cols] = matmul(source, weight[:, cols])
    for i in range(rows // ROWS):
        here = pl.ds(i * ROWS, ROWS)
        value = proj[here, :]
        r = lax.rsqrt(jnp.sum(value * value, axis=1, keepdims=True) + epsilon)
        r_out[here, :] = r
        emb[here, :] = (value * r).astype(BF16)


def passage_kernel(passages, weight, emb, r_out, proj):
    project(passages[...], weight, proj, r_out, emb, OWN)


def passage_side(passages, weight):
    return call(
        passage_kernel, "passage_side",
        (pltpu.HBM((OWN, WIDTH), BF16), pltpu.HBM((OWN, 1), F32)),
        [VMEM, VMEM],
        (VMEM, VMEM),
        [pltpu.VMEM((OWN, WIDTH), F32)],
        16, 1_000, 1_000,
        passages, weight,
    )


def flat(value):
    return jnp.concatenate([value[k : k + 1] for k in range(X)], axis=1)


def score_kernel(
    place, tiles, weight, emb_own, emb_sib, q_emb, q_r, exponent, send, pos_row, p_emb, rows, proj, sems
):
    x, c = place[0], place[1]
    copies = [
        pltpu.make_async_copy(emb_own, p_emb.at[pl.ds(0, OWN)], sems.at[0]),
        pltpu.make_async_copy(emb_sib, p_emb.at[pl.ds(OWN, OWN)], sems.at[1]),
    ]
    for copy in copies:
        copy.start()
    lines = [tiles[k, PIECES * ROWS : LINES, :].astype(F32) for k in range(X)]
    pos_name, pos_rest, names = [
        jnp.concatenate([line[i : i + 1] for line in lines], axis=0).astype(jnp.int32) for i in range(3)
    ]
    local = names - x * CHIP_BLOCKS
    turned = local + BLOCKS * c
    turned = jnp.where(turned >= CHIP_BLOCKS, turned - CHIP_BLOCKS, turned)
    slot = jnp.where((local >= 0) & (local < CHIP_BLOCKS), turned, -1)
    lane = lax.broadcasted_iota(jnp.int32, (X, ROWS), 1)
    pos_slot = jnp.full((X, ROWS), -1, jnp.int32)
    for n in range(NAMES):
        of_name = jnp.max(jnp.where(lane == n, slot, -1), axis=1, keepdims=True)
        pos_slot = jnp.where(pos_name == n, of_name, pos_slot)
    pos = flat(jnp.where(pos_slot >= 0, pos_slot * ROWS + pos_rest, -1))
    pos_row[...] = pos

    for k in range(X):
        for j in range(PIECES):
            rows[pl.ds(k * ROWS, ROWS), j * LANES : (j + 1) * LANES] = tiles[k, j * ROWS : (j + 1) * ROWS, :]
    project(rows[...], weight, proj, q_r, q_emb, X * ROWS)
    for copy in copies:
        copy.wait()
    line = lax.broadcasted_iota(jnp.int32, (ROWS, X * ROWS), 0)
    total = jnp.zeros((1, X * ROWS), F32)
    picked = jnp.zeros((1, X * ROWS), F32)
    for h in range(C):
        half = matmul_nt(p_emb[pl.ds(h * OWN, OWN), :], q_emb[...])
        for i in range(BLOCKS):
            b = h * BLOCKS + i
            named = jnp.max(jnp.where(slot == b, 1, 0), axis=1, keepdims=True)
            named = flat(jnp.broadcast_to(named, (X, ROWS)))
            scores = half[i * ROWS : (i + 1) * ROWS] * score_scale
            value = jnp.where(named > 0, jnp.exp(scores), 0.0)
            exponent[pl.ds(b * ROWS, ROWS), :] = value
            total = total + jnp.sum(value, axis=0, keepdims=True)
            picked = picked + jnp.sum(jnp.where(line == pos - b * ROWS, scores, 0.0), axis=0, keepdims=True)
    send[...] = jnp.zeros(send.shape, F32)
    for k in range(X):
        lanes = slice(k * ROWS, (k + 1) * ROWS)
        for d in range(X):
            send[d, k : k + 1, :] = total[:, lanes]
        send[k, X : X + 1, :] = picked[:, lanes]


def score_side(place, tiles, weight, emb_own, emb_sib):
    queries = X * ROWS
    passages = CHIP_BLOCKS * ROWS
    return call(
        score_kernel, "score_side",
        (
            shape((queries, WIDTH), BF16),
            shape((queries, 1), F32),
            shape((passages, queries), F32),
            shape((X, 8, ROWS), F32),
            shape((1, queries), jnp.int32),
            shape((passages, WIDTH), BF16),
            shape((queries, WIDTH), BF16),
        ),
        [SMEM] + [VMEM] * 2 + [HBM] * 2,
        (VMEM,) * 7,
        [
            pltpu.VMEM((queries, WIDTH), F32),
            pltpu.SemaphoreType.DMA((2,)),
        ],
        SCORE, 2_000_000_000, 8_000_000,
        place, tiles, weight, *in_hbm(emb_own, emb_sib),
    )


def grad_kernel(
    place, recv, pos_row, exponent, q_r, r_own, r_sib, q_emb, p_emb, q_rows, own, sib,
    losses, g0, g1, g2, g3, emb_mine, r_mine, p_grad_own, p_grad_sib, backs_here, passages, w_there,
    dscore, q_grad, p_grad, backs, sems,
):
    x, c = place[0], place[1]
    queries = X * ROWS
    copies = [
        pltpu.make_async_copy(own, passages.at[pl.ds(0, OWN)], sems.at[0]),
        pltpu.make_async_copy(sib, passages.at[pl.ds(OWN, OWN)], sems.at[1]),
    ]
    for copy in copies:
        copy.start()
    total = recv[0] + recv[1] + recv[2] + recv[3]
    mine = jnp.zeros((1, ROWS), F32)
    for k in range(X):
        mine = mine + jnp.where(x == k, total[k : k + 1], 0.0)
    losses[...] = jnp.log(mine) - total[X : X + 1]
    inverse = 1.0 / flat(total)
    pos = pos_row[...]
    line = lax.broadcasted_iota(jnp.int32, (ROWS, queries), 0)
    for b in range(CHIP_BLOCKS):
        block = pl.ds(b * ROWS, ROWS)
        target = jnp.where(line == pos - b * ROWS, 1.0, 0.0)
        dscore[block, :] = (exponent[block, :] * inverse - target).astype(BF16)

    def keep(rows, emb, r, grad):
        value = back_of(emb, r * score_scale, grad).astype(BF16)
        for h in range(C):
            backs[h, rows, :] = value[:, h * HALF : (h + 1) * HALF]

    for j in range(WIDTH // PART):
        cols = pl.ds(j * PART, PART)
        q_grad[:, cols] = matmul_tn(dscore[...], p_emb[:, cols])
    for j in range(WIDTH // PART):
        cols = pl.ds(j * PART, PART)
        p_grad[:, cols] = matmul(dscore[...], q_emb[:, cols])
    for k in range(X):
        rows = pl.ds(k * ROWS, ROWS)
        keep(rows, q_emb[rows, :], q_r[rows, :], q_grad[rows, :])
    for k, out in enumerate((g0, g1, g2, g3)):
        rows = pl.ds(pl.multiple_of(lax.rem(x + k, X) * ROWS, ROWS), ROWS)
        out[...] = q_grad[rows, :].astype(out.dtype)
    rows = pl.ds(pl.multiple_of(x * ROWS, ROWS), ROWS)
    emb_mine[...] = q_emb[rows, :]
    r_mine[...] = q_r[rows, :]
    for b in range(CHIP_BLOCKS):
        rows = pl.ds(b * ROWS, ROWS)
        first = b < BLOCKS
        near = pl.ds((b % BLOCKS) * ROWS, ROWS)
        grad = p_grad[rows, :]
        (p_grad_own if first else p_grad_sib)[near, :] = grad.astype(F32 if first else BF16)
        r = (r_own if first else r_sib)[near, :]
        keep(pl.ds(queries + b * ROWS, ROWS), p_emb[rows, :], r, grad)
    for copy in copies:
        copy.wait()
    weight_terms(q_rows, passages, backs.at[1 - c], w_there)
    backs_here[...] = backs[c]


def weight_terms(q_rows, passages, backs, out):
    for j in range(WIDTH // PART):
        cols = pl.ds(j * PART, PART)
        hidden = jnp.concatenate([q_rows[:, cols], passages[:, cols]], axis=0)
        out[cols, :] = matmul_tn(hidden, backs[...]).astype(out.dtype)


def grad_side(*args, own, sib):
    queries = X * ROWS
    passages = CHIP_BLOCKS * ROWS
    tile = shape((ROWS, WIDTH), BF16)
    return call(
        grad_kernel, "grad_side",
        (
            shape((1, ROWS), F32),
            pltpu.HBM((ROWS, WIDTH), F32), tile, tile, tile,
            pltpu.HBM((ROWS, WIDTH), BF16),
            pltpu.HBM((ROWS, 1), F32),
            shape((OWN, WIDTH), F32),
            shape((OWN, WIDTH), BF16),
            shape((queries + passages, HALF), BF16),
            shape((passages, WIDTH), BF16),
            shape((WIDTH, HALF), BF16),
        ),
        [SMEM] + [VMEM] * 9 + [HBM] * 2,
        (VMEM,) * 12,
        [
            pltpu.VMEM((passages, queries), BF16),
            pltpu.VMEM((queries, WIDTH), F32),
            pltpu.VMEM((passages, WIDTH), F32),
            pltpu.VMEM((C, queries + passages, HALF), BF16),
            pltpu.SemaphoreType.DMA((2,)),
        ],
        GRAD, 3_000_000_000, 14_000_000,
        *args, *in_hbm(own, sib),
    )


def weight_kernel(backs, q_rows, passages, out):
    weight_terms(q_rows, passages, backs, out)


def weight_here(backs, q_rows, passages):
    return call(
        weight_kernel, "weight_here",
        shape((WIDTH, HALF), F32),
        [VMEM] * 3,
        VMEM,
        [],
        24, 1_350_000_000, 6_000_000,
        backs, q_rows, passages,
    )


def spread_kernel(here, there, out, held, sems):
    own_rows = WIDTH // (Z * Y)
    lanes = HALF // X
    copies = []
    for y in range(Y):
        for z in range(Z):
            rows = pl.ds((z * Y + y) * own_rows, own_rows)
            value = (here[rows, :] + there[rows, :].astype(F32)).astype(BF16)
            for x in range(X):
                held[y * X + x, z] = value[:, x * lanes : (x + 1) * lanes]
        part = pl.ds(y * X, X)
        copies.append(pltpu.make_async_copy(held.at[part], out.at[part], sems.at[y]))
        copies[-1].start()
    for copy in copies:
        copy.wait()


def spread(here, there):
    dims = (Y * X, Z, WIDTH // (Z * Y), HALF // X)
    return call(
        spread_kernel, "spread",
        pltpu.HBM(dims, BF16),
        [VMEM, VMEM],
        HBM,
        [pltpu.VMEM(dims, BF16), pltpu.SemaphoreType.DMA((Y,))],
        16, 500_000, 4_000_000,
        here, there,
    )


def sum_kernel(pieces, out):
    total = pieces[0].astype(F32)
    for k in range(1, pieces.shape[0]):
        total = total + pieces[k].astype(F32)
    out[...] = total.astype(BF16)


def sum_pieces(pieces):
    return call(
        sum_kernel, "sum_pieces", shape(pieces.shape[1:], BF16), [VMEM], VMEM, [], 8, 500_000, 1_000_000, pieces
    )


def last_sum_kernel(pieces, out):
    total = pieces[0].astype(F32)
    for k in range(1, Z):
        total = total + pieces[k].astype(F32)
    total = total * (1.0 / (Z * Y * X * C))
    for d in range(X * C):
        out[d] = total


def last_sum(pieces):
    dims = (X * C,) + pieces.shape[1:]
    return call(
        last_sum_kernel, "last_sum", shape(dims, F32), [VMEM], VMEM, [], 8, 50_000, 100_000, pieces
    )


def lay_kernel(pieces, out):
    lanes = HALF // X
    for x in range(X):
        for c in range(C):
            out[:, c * HALF + x * lanes : c * HALF + (x + 1) * lanes] = pieces[x * C + c]


def lay(pieces):
    dims = (WIDTH // (Z * Y), WIDTH)
    return call(lay_kernel, "lay", shape(dims, F32), [VMEM], VMEM, [], 8, 0, 200_000, pieces)


def hidden_kernel(*refs):
    *terms, emb, r, weight, out = refs
    grad = terms[0][...]
    for term in terms[1:]:
        grad = grad + term[...].astype(F32)
    back = back_of(emb[...], r[...] * score_scale, grad).astype(BF16)
    for j in range(WIDTH // PART):
        cols = pl.ds(j * PART, PART)
        out[:, cols] = matmul_nt(back, weight[cols, :]).astype(BF16)


def hidden_grad(terms, emb, r, weight):
    rows = emb.shape[0]
    return call(
        hidden_kernel, "hidden_grad",
        shape((rows, WIDTH), BF16),
        [VMEM] * (len(terms) + 3),
        VMEM,
        [],
        24, 2 * rows * WIDTH * WIDTH, 2_000_000 + rows * 10_000,
        *in_hbm(terms[0]), *terms[1:], *in_hbm(emb, r), weight,
    )


def body(queries, passages, weight, pairs, positive):
    x = lax.axis_index("x")
    c = lax.axis_index("c")
    place = jnp.stack([x, c]).astype(jnp.int32)

    packed = pack(queries, positive, pairs)
    tiles = exchange(packed, "x")
    passages, weight, _ = lax.optimization_barrier((passages, weight, packed))
    emb_own, r_own = passage_side(passages, weight)
    outgoing, _ = lax.optimization_barrier((passages, emb_own))
    sibling = lax.ppermute(outgoing, "c", SWAP)
    emb_sib, r_sib = passage_side(sibling, weight)

    q_emb, q_r, exponent, send, pos_row, p_emb, q_rows = score_side(place, tiles, weight, emb_own, emb_sib)
    recv = exchange(send, "x")
    losses, g0, g1, g2, g3, emb_mine, r_mine, p_grad, p_grad_sib, backs, hidden, w_there = grad_side(
        place, recv, pos_row, exponent, q_r, r_own, r_sib, q_emb, p_emb, q_rows, own=passages, sib=sibling
    )

    w_there = lax.ppermute(w_there, "c", SWAP)
    w = spread(weight_here(backs, q_rows, hidden), w_there)
    (p_grad_sib, g1, g3), w = lax.optimization_barrier(((p_grad_sib, g1, g3), w))
    p_grad_sib = lax.ppermute(p_grad_sib, "c", SWAP)
    passage_grad = hidden_grad((p_grad, p_grad_sib), emb_own, r_own, weight)
    g1 = lax.ppermute(g1, "x", shift(X - 1))
    g3 = lax.ppermute(g3, "x", shift(X - 3))

    w = sum_pieces(exchange(w, ("y", "x")))
    w, g2, g1, g3, passage_grad = lax.optimization_barrier((w, g2, g1, g3, passage_grad))
    g2 = lax.ppermute(g2, "x", shift(X - 2))
    query_grad = hidden_grad((g0, g1, g2, g3), emb_mine, r_mine, weight)
    w = last_sum(exchange(w, "z"))
    weight_grad = lay(exchange(w, ("x", "c")))
    return losses.reshape(ROWS), query_grad, passage_grad, weight_grad


def solution(mesh):
    torus = Mesh(mesh.devices.reshape(Z, Y, X, C), ("z", "y", "x", "c"))
    every = ("z", "y", "x", "c")
    return jax.shard_map(
        body,
        mesh=torus,
        in_specs=(P(every, None), P(every, None), P(), P(every, None), P(every)),
        out_specs=(P(every), P(every, None), P(every, None), P(("z", "y"), None)),
        check_vma=False,
    )
```

```python
import jax
import jax.numpy as jnp
from jax import lax
from jax.experimental import pallas as pl
from jax.experimental.pallas import tpu as pltpu
from jax.sharding import Mesh, PartitionSpec as P

score_scale = 50.0
epsilon = 1e-06

X, C, Y, Z = 4, 2, 4, 16
SWAP = ((0, 1), (1, 0))
ROWS = 128
WIDTH = 1024
OWN = 384
BLOCKS = OWN // ROWS
CHIP_BLOCKS = BLOCKS * C
NAMES = 8
LANES = 128
PIECES = WIDTH // LANES
EXTRA = 16
LINES = PIECES * ROWS + EXTRA
HALF = WIDTH // C
PART = 512
HBM = pl.BlockSpec(memory_space=pltpu.HBM)
VMEM = pl.BlockSpec(memory_space=pltpu.VMEM)
SMEM = pl.BlockSpec(memory_space=pltpu.SMEM)
F32, BF16 = jnp.float32, jnp.bfloat16
SCORE = 24
GRAD = 32


def shift(k):
    return tuple(((i + k) % X, i) for i in range(X))


def exchange(value, axis):
    return lax.all_to_all(value, axis, split_axis=0, concat_axis=0, tiled=True)


def matmul(a, b):
    return jnp.dot(a, b, preferred_element_type=F32)


def matmul_tn(a, b):
    return lax.dot_general(a, b, (((0,), (0,)), ((), ())), preferred_element_type=F32)


def matmul_nt(a, b):
    return lax.dot_general(a, b, (((1,), (1,)), ((), ())), preferred_element_type=F32)


def back_of(emb, r, grad):
    emb = emb.astype(F32)
    inner = jnp.sum(emb * grad, axis=-1, keepdims=True)
    return r * (grad - inner * emb)


def params(mib):
    return pltpu.CompilerParams(vmem_limit_bytes=mib << 20)


def in_hbm(*values):
    return [pltpu.with_memory_space_constraint(value, pltpu.HBM) for value in values]


def shape(dims, dtype):
    return jax.ShapeDtypeStruct(dims, dtype)


def call(kernel, name, out_shape, in_specs, out_specs, scratch, mib, flops, moved, *args):
    return pl.pallas_call(
        kernel,
        name=name,
        out_shape=out_shape,
        in_specs=in_specs,
        out_specs=out_specs,
        scratch_shapes=scratch,
        compiler_params=params(mib),
        cost_estimate=pl.CostEstimate(flops=flops, bytes_accessed=moved, transcendentals=0),
    )(*args)


def pack_kernel(queries, positive, pairs, out, pos, names, rows, wide, packed, sems):
    inner = [
        pltpu.make_async_copy(queries, rows, sems.at[X]),
        pltpu.make_async_copy(positive, pos, sems.at[X + 1]),
        pltpu.make_async_copy(pairs, names, sems.at[X + 2]),
    ]
    for copy in inner:
        copy.start()
    wide[...] = jnp.full(wide.shape, 255.0, F32)
    inner[1].wait()
    inner[2].wait()
    index = pos[...]
    wide[0:1, :] = (index >> 7).astype(F32)
    wide[1:2, :] = (index & 127).astype(F32)
    wide[2:3, 0:NAMES] = names[...].astype(F32)
    packed[pl.ds(PIECES * ROWS, EXTRA), :] = wide[...].astype(BF16)
    inner[0].wait()
    for j in range(PIECES):
        packed[pl.ds(j * ROWS, ROWS), :] = rows[:, j * LANES : (j + 1) * LANES]
    copies = [pltpu.make_async_copy(packed, out.at[d], sems.at[d]) for d in range(X)]
    for copy in copies:
        copy.start()
    for copy in copies:
        copy.wait()


def pack(queries, positive, pairs):
    return call(
        pack_kernel, "pack",
        pltpu.HBM((X, LINES, LANES), BF16),
        [HBM, HBM, HBM],
        HBM,
        [
            pltpu.VMEM((1, ROWS), jnp.int32),
            pltpu.VMEM((1, NAMES), jnp.int32),
            pltpu.VMEM((ROWS, WIDTH), BF16),
            pltpu.VMEM((EXTRA, LANES), F32),
            pltpu.VMEM((LINES, LANES), BF16),
            pltpu.SemaphoreType.DMA((X + 3,)),
        ],
        4, 0, 1_400_000,
        *in_hbm(queries, positive.reshape(1, ROWS), pairs),
    )


def project(source, weight, proj, r_out, emb, rows):
    for j in range(WIDTH // PART):
        cols = pl.ds(j * PART, PART)
        proj[:, cols] = matmul(source, weight[:, cols])
    for i in range(rows // ROWS):
        here = pl.ds(i * ROWS, ROWS)
        value = proj[here, :]
        r = lax.rsqrt(jnp.sum(value * value, axis=1, keepdims=True) + epsilon)
        r_out[here, :] = r
        emb[here, :] = (value * r).astype(BF16)


def passage_kernel(passages, weight, emb, r_out, proj):
    project(passages[...], weight, proj, r_out, emb, OWN)


def passage_side(passages, weight):
    return call(
        passage_kernel, "passage_side",
        (pltpu.HBM((OWN, WIDTH), BF16), pltpu.HBM((OWN, 1), F32)),
        [VMEM, VMEM],
        (VMEM, VMEM),
        [pltpu.VMEM((OWN, WIDTH), F32)],
        16, 1_000, 1_000,
        passages, weight,
    )


def flat(value):
    return jnp.concatenate([value[k : k + 1] for k in range(X)], axis=1)


def score_kernel(
    place, tiles, weight, emb_own, emb_sib, own, sib,
    q_emb, q_r, exponent, send, pos_row, p_emb, rows, passages, emb_mine, r_mine,
    proj, sems,
):
    x, c = place[0], place[1]
    copies = [
        pltpu.make_async_copy(emb_own, p_emb.at[pl.ds(0, OWN)], sems.at[0]),
        pltpu.make_async_copy(emb_sib, p_emb.at[pl.ds(OWN, OWN)], sems.at[1]),
    ]
    late = [
        pltpu.make_async_copy(own, passages.at[pl.ds(0, OWN)], sems.at[2]),
        pltpu.make_async_copy(sib, passages.at[pl.ds(OWN, OWN)], sems.at[3]),
    ]
    for copy in copies + late:
        copy.start()
    lines = [tiles[k, PIECES * ROWS : LINES, :].astype(F32) for k in range(X)]
    pos_name, pos_rest, names = [
        jnp.concatenate([line[i : i + 1] for line in lines], axis=0).astype(jnp.int32) for i in range(3)
    ]
    local = names - x * CHIP_BLOCKS
    turned = local + BLOCKS * c
    turned = jnp.where(turned >= CHIP_BLOCKS, turned - CHIP_BLOCKS, turned)
    slot = jnp.where((local >= 0) & (local < CHIP_BLOCKS), turned, -1)
    lane = lax.broadcasted_iota(jnp.int32, (X, ROWS), 1)
    pos_slot = jnp.full((X, ROWS), -1, jnp.int32)
    for n in range(NAMES):
        of_name = jnp.max(jnp.where(lane == n, slot, -1), axis=1, keepdims=True)
        pos_slot = jnp.where(pos_name == n, of_name, pos_slot)
    pos = flat(jnp.where(pos_slot >= 0, pos_slot * ROWS + pos_rest, -1))
    pos_row[...] = pos

    for k in range(X):
        for j in range(PIECES):
            rows[pl.ds(k * ROWS, ROWS), j * LANES : (j + 1) * LANES] = tiles[k, j * ROWS : (j + 1) * ROWS, :]
    project(rows[...], weight, proj, q_r, q_emb, X * ROWS)
    for copy in copies:
        copy.wait()
    mine = pl.ds(pl.multiple_of(x * ROWS, ROWS), ROWS)
    kept = [
        pltpu.make_async_copy(q_emb.at[mine], emb_mine, sems.at[4]),
        pltpu.make_async_copy(q_r.at[mine], r_mine, sems.at[5]),
    ]
    for copy in kept:
        copy.start()
    line = lax.broadcasted_iota(jnp.int32, (ROWS, X * ROWS), 0)
    total = jnp.zeros((1, X * ROWS), F32)
    picked = jnp.zeros((1, X * ROWS), F32)
    for h in range(C):
        half = matmul_nt(p_emb[pl.ds(h * OWN, OWN), :], q_emb[...])
        for i in range(BLOCKS):
            b = h * BLOCKS + i
            named = jnp.max(jnp.where(slot == b, 1, 0), axis=1, keepdims=True)
            named = flat(jnp.broadcast_to(named, (X, ROWS)))
            scores = half[i * ROWS : (i + 1) * ROWS] * score_scale
            value = jnp.where(named > 0, jnp.exp(scores), 0.0)
            exponent[pl.ds(b * ROWS, ROWS), :] = value
            total = total + jnp.sum(value, axis=0, keepdims=True)
            picked = picked + jnp.sum(jnp.where(line == pos - b * ROWS, scores, 0.0), axis=0, keepdims=True)
    send[...] = jnp.zeros(send.shape, F32)
    for k in range(X):
        lanes = slice(k * ROWS, (k + 1) * ROWS)
        for d in range(X):
            send[d, k : k + 1, :] = total[:, lanes]
        send[k, X : X + 1, :] = picked[:, lanes]
    for copy in late + kept:
        copy.wait()


def score_side(place, tiles, weight, emb_own, emb_sib, own, sib):
    queries = X * ROWS
    passages = CHIP_BLOCKS * ROWS
    return call(
        score_kernel, "score_side",
        (
            shape((queries, WIDTH), BF16),
            shape((queries, 1), F32),
            shape((passages, queries), F32),
            shape((X, 8, ROWS), F32),
            shape((1, queries), jnp.int32),
            shape((passages, WIDTH), BF16),
            shape((queries, WIDTH), BF16),
            shape((passages, WIDTH), BF16),
            pltpu.HBM((ROWS, WIDTH), BF16),
            pltpu.HBM((ROWS, 1), F32),
        ),
        [SMEM] + [VMEM] * 2 + [HBM] * 4,
        (VMEM,) * 8 + (HBM,) * 2,
        [
            pltpu.VMEM((queries, WIDTH), F32),
            pltpu.SemaphoreType.DMA((6,)),
        ],
        SCORE, 2_000_000_000, 8_000_000,
        place, tiles, weight, *in_hbm(emb_own, emb_sib, own, sib),
    )


def grad_kernel(
    place, recv, pos_row, exponent, q_r, r_own, r_sib, q_emb, p_emb, q_rows, passages,
    losses, g0, g1, g2, g3, p_grad_own, p_grad_sib, backs_here, w_there,
    dscore, q_grad, p_grad, backs,
):
    x, c = place[0], place[1]
    queries = X * ROWS
    total = recv[0] + recv[1] + recv[2] + recv[3]
    mine = jnp.zeros((1, ROWS), F32)
    for k in range(X):
        mine = mine + jnp.where(x == k, total[k : k + 1], 0.0)
    losses[...] = jnp.log(mine) - total[X : X + 1]
    inverse = 1.0 / flat(total)
    pos = pos_row[...]
    line = lax.broadcasted_iota(jnp.int32, (ROWS, queries), 0)
    for b in range(CHIP_BLOCKS):
        block = pl.ds(b * ROWS, ROWS)
        target = jnp.where(line == pos - b * ROWS, 1.0, 0.0)
        dscore[block, :] = (exponent[block, :] * inverse - target).astype(BF16)

    def keep(rows, emb, r, grad):
        value = back_of(emb, r * score_scale, grad).astype(BF16)
        low, high = value[:, :HALF], value[:, HALF:]
        backs[0, rows, :] = jnp.where(c == 0, low, high)
        backs[1, rows, :] = jnp.where(c == 0, high, low)

    for j in range(WIDTH // HALF):
        cols = pl.ds(j * HALF, HALF)
        q_grad[:, cols] = matmul_tn(dscore[...], p_emb[:, cols])
    for j in range(WIDTH // HALF):
        cols = pl.ds(j * HALF, HALF)
        p_grad[:, cols] = matmul(dscore[...], q_emb[:, cols])
    for k in range(X):
        rows = pl.ds(k * ROWS, ROWS)
        keep(rows, q_emb[rows, :], q_r[rows, :], q_grad[rows, :])
    for k, out in enumerate((g0, g1, g2, g3)):
        rows = pl.ds(pl.multiple_of(lax.rem(x + k, X) * ROWS, ROWS), ROWS)
        out[...] = q_grad[rows, :].astype(out.dtype)
    for b in range(CHIP_BLOCKS):
        rows = pl.ds(b * ROWS, ROWS)
        first = b < BLOCKS
        near = pl.ds((b % BLOCKS) * ROWS, ROWS)
        grad = p_grad[rows, :]
        (p_grad_own if first else p_grad_sib)[near, :] = grad.astype(F32 if first else BF16)
        r = (r_own if first else r_sib)[near, :]
        keep(pl.ds(queries + b * ROWS, ROWS), p_emb[rows, :], r, grad)
    weight_terms(q_rows, passages, backs.at[1], w_there)
    backs_here[...] = backs[0]


def weight_terms(q_rows, passages, backs, out):
    for j in range(WIDTH // HALF):
        cols = pl.ds(j * HALF, HALF)
        hidden = jnp.concatenate([q_rows[:, cols], passages[:, cols]], axis=0)
        out[cols, :] = matmul_tn(hidden, backs[...]).astype(out.dtype)


def grad_side(*args):
    queries = X * ROWS
    passages = CHIP_BLOCKS * ROWS
    tile = shape((ROWS, WIDTH), BF16)
    return call(
        grad_kernel, "grad_side",
        (
            shape((1, ROWS), F32),
            tile, tile, tile, tile,
            shape((OWN, WIDTH), F32),
            shape((OWN, WIDTH), BF16),
            shape((queries + passages, HALF), BF16),
            shape((WIDTH, HALF), BF16),
        ),
        [SMEM] + [VMEM] * 10,
        (VMEM,) * 9,
        [
            pltpu.VMEM((passages, queries), BF16),
            pltpu.VMEM((queries, WIDTH), F32),
            pltpu.VMEM((passages, WIDTH), F32),
            pltpu.VMEM((C, queries + passages, HALF), BF16),
        ],
        GRAD, 3_000_000_000, 14_000_000,
        *args,
    )


def weight_kernel(backs, q_rows, passages, out):
    weight_terms(q_rows, passages, backs, out)


def weight_here(backs, q_rows, passages):
    return call(
        weight_kernel, "weight_here",
        shape((WIDTH, HALF), F32),
        [VMEM] * 3,
        VMEM,
        [],
        24, 1_350_000_000, 6_000_000,
        backs, q_rows, passages,
    )


def spread_kernel(here, there, out, held, sems):
    own_rows = WIDTH // (Z * Y)
    lanes = HALF // X
    copies = []
    for y in range(Y):
        for z in range(Z):
            rows = pl.ds((z * Y + y) * own_rows, own_rows)
            value = (here[rows, :] + there[rows, :].astype(F32)).astype(BF16)
            for x in range(X):
                held[y * X + x, z] = value[:, x * lanes : (x + 1) * lanes]
        part = pl.ds(y * X, X)
        copies.append(pltpu.make_async_copy(held.at[part], out.at[part], sems.at[y]))
        copies[-1].start()
    for copy in copies:
        copy.wait()


def spread(here, there):
    dims = (Y * X, Z, WIDTH // (Z * Y), HALF // X)
    return call(
        spread_kernel, "spread",
        pltpu.HBM(dims, BF16),
        [VMEM, VMEM],
        HBM,
        [pltpu.VMEM(dims, BF16), pltpu.SemaphoreType.DMA((Y,))],
        16, 500_000, 4_000_000,
        here, there,
    )


def sum_kernel(pieces, out):
    total = pieces[0].astype(F32)
    for k in range(1, pieces.shape[0]):
        total = total + pieces[k].astype(F32)
    out[...] = total.astype(BF16)


def sum_pieces(pieces):
    return call(
        sum_kernel, "sum_pieces", shape(pieces.shape[1:], BF16), [VMEM], VMEM, [], 8, 500_000, 1_000_000, pieces
    )


def last_sum_kernel(pieces, out):
    total = pieces[0].astype(F32)
    for k in range(1, Z):
        total = total + pieces[k].astype(F32)
    total = total * (1.0 / (Z * Y * X * C))
    for d in range(X * C):
        out[d] = total


def last_sum(pieces):
    dims = (X * C,) + pieces.shape[1:]
    return call(
        last_sum_kernel, "last_sum", shape(dims, F32), [VMEM], VMEM, [], 8, 50_000, 100_000, pieces
    )


def lay_kernel(pieces, out):
    lanes = HALF // X
    for x in range(X):
        for c in range(C):
            out[:, c * HALF + x * lanes : c * HALF + (x + 1) * lanes] = pieces[x * C + c]


def lay(pieces):
    dims = (WIDTH // (Z * Y), WIDTH)
    return call(lay_kernel, "lay", shape(dims, F32), [VMEM], VMEM, [], 8, 0, 200_000, pieces)


def hidden_kernel(*refs):
    *terms, emb, r, weight, out = refs
    grad = terms[0][...].astype(F32)
    for term in terms[1:]:
        grad = grad + term[...].astype(F32)
    back = back_of(emb[...], r[...] * score_scale, grad).astype(BF16)
    for j in range(WIDTH // PART):
        cols = pl.ds(j * PART, PART)
        out[:, cols] = matmul_nt(back, weight[cols, :]).astype(BF16)


def hidden_grad(terms, emb, r, weight):
    rows = emb.shape[0]
    return call(
        hidden_kernel, "hidden_grad",
        shape((rows, WIDTH), BF16),
        [VMEM] * (len(terms) + 3),
        VMEM,
        [],
        24, 2 * rows * WIDTH * WIDTH, 2_000_000 + rows * 10_000,
        *terms, *in_hbm(emb, r), weight,
    )


def body(queries, passages, weight, pairs, positive):
    x = lax.axis_index("x")
    c = lax.axis_index("c")
    place = jnp.stack([x, c]).astype(jnp.int32)

    packed = pack(queries, positive, pairs)
    tiles = exchange(packed, "x")
    passages, weight, _ = lax.optimization_barrier((passages, weight, packed))
    emb_own, r_own = passage_side(passages, weight)
    outgoing, _ = lax.optimization_barrier((passages, emb_own))
    sibling = lax.ppermute(outgoing, "c", SWAP)
    emb_sib, r_sib = passage_side(sibling, weight)

    q_emb, q_r, exponent, send, pos_row, p_emb, q_rows, hidden, emb_mine, r_mine = score_side(
        place, tiles, weight, emb_own, emb_sib, passages, sibling
    )
    recv = exchange(send, "x")
    losses, g0, g1, g2, g3, p_grad, p_grad_sib, backs, w_there = grad_side(
        place, recv, pos_row, exponent, q_r, r_own, r_sib, q_emb, p_emb, q_rows, hidden
    )

    w_there = lax.ppermute(w_there, "c", SWAP)
    w = spread(weight_here(backs, q_rows, hidden), w_there)
    (p_grad_sib, g1, g3), w = lax.optimization_barrier(((p_grad_sib, g1, g3), w))
    p_grad_sib = lax.ppermute(p_grad_sib, "c", SWAP)
    passage_grad = hidden_grad((p_grad, p_grad_sib), emb_own, r_own, weight)
    g1 = lax.ppermute(g1, "x", shift(X - 1))
    g3 = lax.ppermute(g3, "x", shift(X - 3))

    w = sum_pieces(exchange(w, ("y", "x")))
    w, g2, g1, g3, passage_grad = lax.optimization_barrier((w, g2, g1, g3, passage_grad))
    g2 = lax.ppermute(g2, "x", shift(X - 2))
    query_grad = hidden_grad((g0, g1, g2, g3), emb_mine, r_mine, weight)
    w = last_sum(exchange(w, "z"))
    weight_grad = lay(exchange(w, ("x", "c")))
    return losses.reshape(ROWS), query_grad, passage_grad, weight_grad


def solution(mesh):
    torus = Mesh(mesh.devices.reshape(Z, Y, X, C), ("z", "y", "x", "c"))
    every = ("z", "y", "x", "c")
    return jax.shard_map(
        body,
        mesh=torus,
        in_specs=(P(every, None), P(every, None), P(), P(every, None), P(every)),
        out_specs=(P(every), P(every, None), P(every, None), P(("z", "y"), None)),
        check_vma=False,
    )
```

```python
import jax
import jax.numpy as jnp
from jax import lax
from jax.experimental import pallas as pl
from jax.experimental.pallas import tpu as pltpu
from jax.sharding import Mesh, PartitionSpec as P

score_scale = 50.0
epsilon = 1e-06

X, C, Y, Z = 4, 2, 4, 16
SWAP = ((0, 1), (1, 0))
ROWS = 128
WIDTH = 1024
OWN = 384
BLOCKS = OWN // ROWS
CHIP_BLOCKS = BLOCKS * C
NAMES = 8
LANES = 128
PIECES = WIDTH // LANES
EXTRA = 16
LINES = PIECES * ROWS + EXTRA
HALF = WIDTH // C
PART = 512
HBM = pl.BlockSpec(memory_space=pltpu.HBM)
VMEM = pl.BlockSpec(memory_space=pltpu.VMEM)
SMEM = pl.BlockSpec(memory_space=pltpu.SMEM)
F32, BF16 = jnp.float32, jnp.bfloat16
SCORE = 24
GRAD = 32


def shift(k):
    return tuple(((i + k) % X, i) for i in range(X))


def exchange(value, axis):
    return lax.all_to_all(value, axis, split_axis=0, concat_axis=0, tiled=True)


def matmul(a, b):
    return jnp.dot(a, b, preferred_element_type=F32)


def matmul_tn(a, b):
    return lax.dot_general(a, b, (((0,), (0,)), ((), ())), preferred_element_type=F32)


def matmul_nt(a, b):
    return lax.dot_general(a, b, (((1,), (1,)), ((), ())), preferred_element_type=F32)


def back_of(emb, r, grad):
    emb = emb.astype(F32)
    inner = jnp.sum(emb * grad, axis=-1, keepdims=True)
    return r * (grad - inner * emb)


def params(mib):
    return pltpu.CompilerParams(vmem_limit_bytes=mib << 20)


def in_hbm(*values):
    return [pltpu.with_memory_space_constraint(value, pltpu.HBM) for value in values]


def shape(dims, dtype):
    return jax.ShapeDtypeStruct(dims, dtype)


def call(kernel, name, out_shape, in_specs, out_specs, scratch, mib, flops, moved, *args):
    return pl.pallas_call(
        kernel,
        name=name,
        out_shape=out_shape,
        in_specs=in_specs,
        out_specs=out_specs,
        scratch_shapes=scratch,
        compiler_params=params(mib),
        cost_estimate=pl.CostEstimate(flops=flops, bytes_accessed=moved, transcendentals=0),
    )(*args)


def pack_kernel(queries, positive, pairs, out, pos, names, rows, wide, packed, sems):
    inner = [
        pltpu.make_async_copy(queries, rows, sems.at[X]),
        pltpu.make_async_copy(positive, pos, sems.at[X + 1]),
        pltpu.make_async_copy(pairs, names, sems.at[X + 2]),
    ]
    for copy in inner:
        copy.start()
    wide[...] = jnp.full(wide.shape, 255.0, F32)
    inner[1].wait()
    inner[2].wait()
    index = pos[...]
    wide[0:1, :] = (index >> 7).astype(F32)
    wide[1:2, :] = (index & 127).astype(F32)
    wide[2:3, 0:NAMES] = names[...].astype(F32)
    packed[pl.ds(PIECES * ROWS, EXTRA), :] = wide[...].astype(BF16)
    inner[0].wait()
    for j in range(PIECES):
        packed[pl.ds(j * ROWS, ROWS), :] = rows[:, j * LANES : (j + 1) * LANES]
    copies = [pltpu.make_async_copy(packed, out.at[d], sems.at[d]) for d in range(X)]
    for copy in copies:
        copy.start()
    for copy in copies:
        copy.wait()


def pack(queries, positive, pairs):
    return call(
        pack_kernel, "pack",
        pltpu.HBM((X, LINES, LANES), BF16),
        [HBM, HBM, HBM],
        HBM,
        [
            pltpu.VMEM((1, ROWS), jnp.int32),
            pltpu.VMEM((1, NAMES), jnp.int32),
            pltpu.VMEM((ROWS, WIDTH), BF16),
            pltpu.VMEM((EXTRA, LANES), F32),
            pltpu.VMEM((LINES, LANES), BF16),
            pltpu.SemaphoreType.DMA((X + 3,)),
        ],
        4, 0, 1_400_000,
        *in_hbm(queries, positive.reshape(1, ROWS), pairs),
    )


def project(source, weight, proj, r_out, emb, rows):
    for j in range(WIDTH // PART):
        cols = pl.ds(j * PART, PART)
        proj[:, cols] = matmul(source, weight[:, cols])
    for i in range(rows // ROWS):
        here = pl.ds(i * ROWS, ROWS)
        value = proj[here, :]
        r = lax.rsqrt(jnp.sum(value * value, axis=1, keepdims=True) + epsilon)
        r_out[here, :] = r
        emb[here, :] = (value * r).astype(BF16)


def passage_kernel(passages, weight, emb, r_out, proj):
    project(passages[...], weight, proj, r_out, emb, OWN)


def passage_side(passages, weight):
    return call(
        passage_kernel, "passage_side",
        (pltpu.HBM((OWN, WIDTH), BF16), pltpu.HBM((OWN, 1), F32)),
        [VMEM, VMEM],
        (VMEM, VMEM),
        [pltpu.VMEM((OWN, WIDTH), F32)],
        16, 1_000, 1_000,
        passages, weight,
    )


def flat(value):
    return jnp.concatenate([value[k : k + 1] for k in range(X)], axis=1)


def score_kernel(
    place, tiles, weight, emb_own, emb_sib, own, sib,
    q_emb, q_r, exponent, send, pos_row, p_emb, rows, passages, emb_mine, r_mine,
    proj, sems,
):
    x, c = place[0], place[1]
    copies = [
        pltpu.make_async_copy(emb_own, p_emb.at[pl.ds(0, OWN)], sems.at[0]),
        pltpu.make_async_copy(emb_sib, p_emb.at[pl.ds(OWN, OWN)], sems.at[1]),
    ]
    late = [
        pltpu.make_async_copy(own, passages.at[pl.ds(0, OWN)], sems.at[2]),
        pltpu.make_async_copy(sib, passages.at[pl.ds(OWN, OWN)], sems.at[3]),
    ]
    for copy in copies + late:
        copy.start()
    lines = [tiles[k, PIECES * ROWS : LINES, :].astype(F32) for k in range(X)]
    pos_name, pos_rest, names = [
        jnp.concatenate([line[i : i + 1] for line in lines], axis=0).astype(jnp.int32) for i in range(3)
    ]
    local = names - x * CHIP_BLOCKS
    turned = local + BLOCKS * c
    turned = jnp.where(turned >= CHIP_BLOCKS, turned - CHIP_BLOCKS, turned)
    slot = jnp.where((local >= 0) & (local < CHIP_BLOCKS), turned, -1)
    lane = lax.broadcasted_iota(jnp.int32, (X, ROWS), 1)
    pos_slot = jnp.full((X, ROWS), -1, jnp.int32)
    for n in range(NAMES):
        of_name = jnp.max(jnp.where(lane == n, slot, -1), axis=1, keepdims=True)
        pos_slot = jnp.where(pos_name == n, of_name, pos_slot)
    pos = flat(jnp.where(pos_slot >= 0, pos_slot * ROWS + pos_rest, -1))
    pos_row[...] = pos

    for k in range(X):
        for j in range(PIECES):
            rows[pl.ds(k * ROWS, ROWS), j * LANES : (j + 1) * LANES] = tiles[k, j * ROWS : (j + 1) * ROWS, :]
    project(rows[...], weight, proj, q_r, q_emb, X * ROWS)
    for copy in copies:
        copy.wait()
    mine = pl.ds(pl.multiple_of(x * ROWS, ROWS), ROWS)
    kept = [
        pltpu.make_async_copy(q_emb.at[mine], emb_mine, sems.at[4]),
        pltpu.make_async_copy(q_r.at[mine], r_mine, sems.at[5]),
    ]
    for copy in kept:
        copy.start()
    line = lax.broadcasted_iota(jnp.int32, (ROWS, X * ROWS), 0)
    total = jnp.zeros((1, X * ROWS), F32)
    picked = jnp.zeros((1, X * ROWS), F32)
    for h in range(C):
        half = matmul_nt(p_emb[pl.ds(h * OWN, OWN), :], q_emb[...])
        for i in range(BLOCKS):
            b = h * BLOCKS + i
            named = jnp.max(jnp.where(slot == b, 1, 0), axis=1, keepdims=True)
            named = flat(jnp.broadcast_to(named, (X, ROWS)))
            scores = half[i * ROWS : (i + 1) * ROWS] * score_scale
            value = jnp.where(named > 0, jnp.exp(scores), 0.0)
            exponent[pl.ds(b * ROWS, ROWS), :] = value
            total = total + jnp.sum(value, axis=0, keepdims=True)
            picked = picked + jnp.sum(jnp.where(line == pos - b * ROWS, scores, 0.0), axis=0, keepdims=True)
    send[...] = jnp.zeros(send.shape, F32)
    for k in range(X):
        lanes = slice(k * ROWS, (k + 1) * ROWS)
        for d in range(X):
            send[d, k : k + 1, :] = total[:, lanes]
        send[k, X : X + 1, :] = picked[:, lanes]
    for copy in late + kept:
        copy.wait()


def score_side(place, tiles, weight, emb_own, emb_sib, own, sib):
    queries = X * ROWS
    passages = CHIP_BLOCKS * ROWS
    return call(
        score_kernel, "score_side",
        (
            shape((queries, WIDTH), BF16),
            shape((queries, 1), F32),
            shape((passages, queries), F32),
            shape((X, 8, ROWS), F32),
            shape((1, queries), jnp.int32),
            shape((passages, WIDTH), BF16),
            shape((queries, WIDTH), BF16),
            shape((passages, WIDTH), BF16),
            pltpu.HBM((ROWS, WIDTH), BF16),
            pltpu.HBM((ROWS, 1), F32),
        ),
        [SMEM] + [VMEM] * 2 + [HBM] * 4,
        (VMEM,) * 8 + (HBM,) * 2,
        [
            pltpu.VMEM((queries, WIDTH), F32),
            pltpu.SemaphoreType.DMA((6,)),
        ],
        SCORE, 2_000_000_000, 8_000_000,
        place, tiles, weight, *in_hbm(emb_own, emb_sib, own, sib),
    )


def grad_kernel(
    place, recv, pos_row, exponent, q_r, r_own, r_sib, q_emb, p_emb, q_rows, passages,
    losses, g0, g1, g2, g3, p_grad_own, p_grad_sib, backs_here, w_there,
    dscore, q_grad, p_grad, backs,
):
    x, c = place[0], place[1]
    queries = X * ROWS
    total = recv[0] + recv[1] + recv[2] + recv[3]
    mine = jnp.zeros((1, ROWS), F32)
    for k in range(X):
        mine = mine + jnp.where(x == k, total[k : k + 1], 0.0)
    losses[...] = jnp.log(mine) - total[X : X + 1]
    inverse = 1.0 / flat(total)
    pos = pos_row[...]
    line = lax.broadcasted_iota(jnp.int32, (ROWS, queries), 0)
    for b in range(CHIP_BLOCKS):
        block = pl.ds(b * ROWS, ROWS)
        target = jnp.where(line == pos - b * ROWS, 1.0, 0.0)
        dscore[block, :] = (exponent[block, :] * inverse - target).astype(BF16)

    def keep(rows, emb, r, grad):
        value = back_of(emb, r * score_scale, grad).astype(BF16)
        low, high = value[:, :HALF], value[:, HALF:]
        backs[0, rows, :] = jnp.where(c == 0, low, high)
        backs[1, rows, :] = jnp.where(c == 0, high, low)

    for j in range(WIDTH // HALF):
        cols = pl.ds(j * HALF, HALF)
        q_grad[:, cols] = matmul_tn(dscore[...], p_emb[:, cols])
    for j in range(WIDTH // HALF):
        cols = pl.ds(j * HALF, HALF)
        p_grad[:, cols] = matmul(dscore[...], q_emb[:, cols])
    for k in range(X):
        rows = pl.ds(k * ROWS, ROWS)
        keep(rows, q_emb[rows, :], q_r[rows, :], q_grad[rows, :])
    for k, out in enumerate((g0, g1, g2, g3)):
        rows = pl.ds(pl.multiple_of(lax.rem(x + k, X) * ROWS, ROWS), ROWS)
        out[...] = q_grad[rows, :].astype(out.dtype)
    for b in range(CHIP_BLOCKS):
        rows = pl.ds(b * ROWS, ROWS)
        first = b < BLOCKS
        near = pl.ds((b % BLOCKS) * ROWS, ROWS)
        grad = p_grad[rows, :]
        (p_grad_own if first else p_grad_sib)[near, :] = grad.astype(F32 if first else BF16)
        r = (r_own if first else r_sib)[near, :]
        keep(pl.ds(queries + b * ROWS, ROWS), p_emb[rows, :], r, grad)
    weight_terms(q_rows, passages, backs.at[1], w_there)
    backs_here[...] = backs[0]


def weight_terms(q_rows, passages, backs, out):
    for j in range(WIDTH // HALF):
        cols = pl.ds(j * HALF, HALF)
        hidden = jnp.concatenate([q_rows[:, cols], passages[:, cols]], axis=0)
        out[cols, :] = matmul_tn(hidden, backs[...]).astype(out.dtype)


def grad_side(*args):
    queries = X * ROWS
    passages = CHIP_BLOCKS * ROWS
    tile = shape((ROWS, WIDTH), BF16)
    return call(
        grad_kernel, "grad_side",
        (
            shape((1, ROWS), F32),
            tile, tile, tile, tile,
            shape((OWN, WIDTH), F32),
            shape((OWN, WIDTH), BF16),
            shape((queries + passages, HALF), BF16),
            shape((WIDTH, HALF), BF16),
        ),
        [SMEM] + [VMEM] * 10,
        (VMEM,) * 9,
        [
            pltpu.VMEM((passages, queries), BF16),
            pltpu.VMEM((queries, WIDTH), F32),
            pltpu.VMEM((passages, WIDTH), F32),
            pltpu.VMEM((C, queries + passages, HALF), BF16),
        ],
        GRAD, 3_000_000_000, 14_000_000,
        *args,
    )


def weight_kernel(backs, q_rows, passages, out):
    weight_terms(q_rows, passages, backs, out)


def weight_here(backs, q_rows, passages):
    return call(
        weight_kernel, "weight_here",
        shape((WIDTH, HALF), F32),
        [VMEM] * 3,
        VMEM,
        [],
        24, 1_350_000_000, 6_000_000,
        backs, q_rows, passages,
    )


def spread_kernel(here, there, out, held, sems):
    own_rows = WIDTH // (Z * Y)
    lanes = HALF // X
    copies = []
    for y in range(Y):
        for z in range(Z):
            rows = pl.ds((z * Y + y) * own_rows, own_rows)
            value = (here[rows, :] + there[rows, :].astype(F32)).astype(BF16)
            for x in range(X):
                held[y * X + x, z] = value[:, x * lanes : (x + 1) * lanes]
        part = pl.ds(y * X, X)
        copies.append(pltpu.make_async_copy(held.at[part], out.at[part], sems.at[y]))
        copies[-1].start()
    for copy in copies:
        copy.wait()


def spread(here, there):
    dims = (Y * X, Z, WIDTH // (Z * Y), HALF // X)
    return call(
        spread_kernel, "spread",
        pltpu.HBM(dims, BF16),
        [VMEM, VMEM],
        HBM,
        [pltpu.VMEM(dims, BF16), pltpu.SemaphoreType.DMA((Y,))],
        16, 500_000, 4_000_000,
        here, there,
    )


def sum_kernel(pieces, out):
    total = pieces[0].astype(F32)
    for k in range(1, pieces.shape[0]):
        total = total + pieces[k].astype(F32)
    out[...] = total.astype(BF16)


def sum_pieces(pieces):
    return call(
        sum_kernel, "sum_pieces", shape(pieces.shape[1:], BF16), [VMEM], VMEM, [], 8, 500_000, 1_000_000, pieces
    )


def last_sum_kernel(pieces, out):
    total = pieces[0].astype(F32)
    for k in range(1, Z):
        total = total + pieces[k].astype(F32)
    total = total * (1.0 / (Z * Y * X * C))
    for d in range(X * C):
        out[d] = total


def last_sum(pieces):
    dims = (X * C,) + pieces.shape[1:]
    return call(
        last_sum_kernel, "last_sum", shape(dims, F32), [VMEM], VMEM, [], 8, 50_000, 100_000, pieces
    )


def lay_kernel(pieces, out):
    lanes = HALF // X
    for x in range(X):
        for c in range(C):
            out[:, c * HALF + x * lanes : c * HALF + (x + 1) * lanes] = pieces[x * C + c]


def lay(pieces):
    dims = (WIDTH // (Z * Y), WIDTH)
    return call(lay_kernel, "lay", shape(dims, F32), [VMEM], VMEM, [], 8, 0, 200_000, pieces)


def hidden_kernel(*refs):
    *terms, emb, r, weight, out = refs
    grad = terms[0][...].astype(F32)
    for term in terms[1:]:
        grad = grad + term[...].astype(F32)
    back = back_of(emb[...], r[...] * score_scale, grad).astype(BF16)
    for j in range(WIDTH // PART):
        cols = pl.ds(j * PART, PART)
        out[:, cols] = matmul_nt(back, weight[cols, :]).astype(BF16)


def hidden_grad(terms, emb, r, weight, far=False):
    rows = emb.shape[0]
    return call(
        hidden_kernel, "hidden_grad",
        shape((rows, WIDTH), BF16),
        [VMEM] * (len(terms) + 3),
        VMEM,
        [],
        24, 2 * rows * WIDTH * WIDTH, 2_000_000 + rows * 10_000,
        *(in_hbm(terms[0]) if far else terms[:1]), *terms[1:], *in_hbm(emb, r), weight,
    )


def body(queries, passages, weight, pairs, positive):
    x = lax.axis_index("x")
    c = lax.axis_index("c")
    place = jnp.stack([x, c]).astype(jnp.int32)

    packed = pack(queries, positive, pairs)
    tiles = exchange(packed, "x")
    passages, weight, _ = lax.optimization_barrier((passages, weight, packed))
    emb_own, r_own = passage_side(passages, weight)
    outgoing, _ = lax.optimization_barrier((passages, emb_own))
    sibling = lax.ppermute(outgoing, "c", SWAP)
    emb_sib, r_sib = passage_side(sibling, weight)

    q_emb, q_r, exponent, send, pos_row, p_emb, q_rows, hidden, emb_mine, r_mine = score_side(
        place, tiles, weight, emb_own, emb_sib, passages, sibling
    )
    recv = exchange(send, "x")
    losses, g0, g1, g2, g3, p_grad, p_grad_sib, backs, w_there = grad_side(
        place, recv, pos_row, exponent, q_r, r_own, r_sib, q_emb, p_emb, q_rows, hidden
    )

    w_there = lax.ppermute(w_there, "c", SWAP)
    w = spread(weight_here(backs, q_rows, hidden), w_there)
    (p_grad_sib, g1, g2, g3), w = lax.optimization_barrier(((p_grad_sib, g1, g2, g3), w))
    g2 = lax.ppermute(g2, "x", shift(X - 2))
    g1 = lax.ppermute(g1, "x", shift(X - 1))
    g3 = lax.ppermute(g3, "x", shift(X - 3))
    query_grad = hidden_grad((g0, g1, g2, g3), emb_mine, r_mine, weight)
    p_grad_sib = lax.ppermute(p_grad_sib, "c", SWAP)
    passage_grad = hidden_grad((p_grad, p_grad_sib), emb_own, r_own, weight, far=True)

    w = sum_pieces(exchange(w, ("y", "x")))
    w, passage_grad = lax.optimization_barrier((w, passage_grad))
    w = exchange(w, "z")
    w, query_grad = lax.optimization_barrier((w, query_grad))
    w = last_sum(w)
    weight_grad = lay(exchange(w, ("x", "c")))
    return losses.reshape(ROWS), query_grad, passage_grad, weight_grad


def solution(mesh):
    torus = Mesh(mesh.devices.reshape(Z, Y, X, C), ("z", "y", "x", "c"))
    every = ("z", "y", "x", "c")
    return jax.shard_map(
        body,
        mesh=torus,
        in_specs=(P(every, None), P(every, None), P(), P(every, None), P(every)),
        out_specs=(P(every), P(every, None), P(every, None), P(("z", "y"), None)),
        check_vma=False,
    )
```

```python
import jax
import jax.numpy as jnp
from jax import lax
from jax.experimental import pallas as pl
from jax.experimental.pallas import tpu as pltpu
from jax.sharding import Mesh, PartitionSpec as P

score_scale = 50.0
epsilon = 1e-06

X, C, Y, Z = 4, 2, 4, 16
SWAP = ((0, 1), (1, 0))
ROWS = 128
WIDTH = 1024
OWN = 384
BLOCKS = OWN // ROWS
CHIP_BLOCKS = BLOCKS * C
NAMES = 8
LANES = 128
PIECES = WIDTH // LANES
EXTRA = 16
LINES = PIECES * ROWS + EXTRA
HALF = WIDTH // C
PART = 512
HBM = pl.BlockSpec(memory_space=pltpu.HBM)
VMEM = pl.BlockSpec(memory_space=pltpu.VMEM)
SMEM = pl.BlockSpec(memory_space=pltpu.SMEM)
F32, BF16 = jnp.float32, jnp.bfloat16
SCORE = 24
GRAD = 32


def shift(k):
    return tuple(((i + k) % X, i) for i in range(X))


def exchange(value, axis):
    return lax.all_to_all(value, axis, split_axis=0, concat_axis=0, tiled=True)


def matmul(a, b):
    return jnp.dot(a, b, preferred_element_type=F32)


def matmul_tn(a, b):
    return lax.dot_general(a, b, (((0,), (0,)), ((), ())), preferred_element_type=F32)


def matmul_nt(a, b):
    return lax.dot_general(a, b, (((1,), (1,)), ((), ())), preferred_element_type=F32)


def back_of(emb, r, grad):
    emb = emb.astype(F32)
    inner = jnp.sum(emb * grad, axis=-1, keepdims=True)
    return r * (grad - inner * emb)


def params(mib):
    return pltpu.CompilerParams(vmem_limit_bytes=mib << 20)


def in_hbm(*values):
    return [pltpu.with_memory_space_constraint(value, pltpu.HBM) for value in values]


def shape(dims, dtype):
    return jax.ShapeDtypeStruct(dims, dtype)


def call(kernel, name, out_shape, in_specs, out_specs, scratch, mib, flops, moved, *args):
    return pl.pallas_call(
        kernel,
        name=name,
        out_shape=out_shape,
        in_specs=in_specs,
        out_specs=out_specs,
        scratch_shapes=scratch,
        compiler_params=params(mib),
        cost_estimate=pl.CostEstimate(flops=flops, bytes_accessed=moved, transcendentals=0),
    )(*args)


def pack_kernel(queries, positive, pairs, out, pos, names, rows, wide, packed, sems):
    inner = [
        pltpu.make_async_copy(queries, rows, sems.at[X]),
        pltpu.make_async_copy(positive, pos, sems.at[X + 1]),
        pltpu.make_async_copy(pairs, names, sems.at[X + 2]),
    ]
    for copy in inner:
        copy.start()
    wide[...] = jnp.full(wide.shape, 255.0, F32)
    inner[1].wait()
    inner[2].wait()
    index = pos[...]
    wide[0:1, :] = (index >> 7).astype(F32)
    wide[1:2, :] = (index & 127).astype(F32)
    wide[2:3, 0:NAMES] = names[...].astype(F32)
    packed[pl.ds(PIECES * ROWS, EXTRA), :] = wide[...].astype(BF16)
    inner[0].wait()
    for j in range(PIECES):
        packed[pl.ds(j * ROWS, ROWS), :] = rows[:, j * LANES : (j + 1) * LANES]
    copies = [pltpu.make_async_copy(packed, out.at[d], sems.at[d]) for d in range(X)]
    for copy in copies:
        copy.start()
    for copy in copies:
        copy.wait()


def pack(queries, positive, pairs):
    return call(
        pack_kernel, "pack",
        pltpu.HBM((X, LINES, LANES), BF16),
        [HBM, HBM, HBM],
        HBM,
        [
            pltpu.VMEM((1, ROWS), jnp.int32),
            pltpu.VMEM((1, NAMES), jnp.int32),
            pltpu.VMEM((ROWS, WIDTH), BF16),
            pltpu.VMEM((EXTRA, LANES), F32),
            pltpu.VMEM((LINES, LANES), BF16),
            pltpu.SemaphoreType.DMA((X + 3,)),
        ],
        4, 0, 1_400_000,
        *in_hbm(queries, positive.reshape(1, ROWS), pairs),
    )


def project(source, weight, proj, r_out, emb, rows):
    for j in range(WIDTH // PART):
        cols = pl.ds(j * PART, PART)
        proj[:, cols] = matmul(source, weight[:, cols])
    for i in range(rows // ROWS):
        here = pl.ds(i * ROWS, ROWS)
        value = proj[here, :]
        r = lax.rsqrt(jnp.sum(value * value, axis=1, keepdims=True) + epsilon)
        r_out[here, :] = r
        emb[here, :] = (value * r).astype(BF16)


def passage_kernel(passages, weight, emb, r_out, proj):
    project(passages[...], weight, proj, r_out, emb, OWN)


def passage_side(passages, weight):
    return call(
        passage_kernel, "passage_side",
        (pltpu.HBM((OWN, WIDTH), BF16), pltpu.HBM((OWN, 1), F32)),
        [VMEM, VMEM],
        (VMEM, VMEM),
        [pltpu.VMEM((OWN, WIDTH), F32)],
        16, 1_000, 1_000,
        passages, weight,
    )


def flat(value):
    return jnp.concatenate([value[k : k + 1] for k in range(X)], axis=1)


def score_kernel(
    place, tiles, weight, emb_own, emb_sib, own, sib,
    q_emb, q_r, exponent, send, pos_row, p_emb, rows, passages, emb_mine, r_mine,
    proj, sems,
):
    x, c = place[0], place[1]
    copies = [
        pltpu.make_async_copy(emb_own, p_emb.at[pl.ds(0, OWN)], sems.at[0]),
        pltpu.make_async_copy(emb_sib, p_emb.at[pl.ds(OWN, OWN)], sems.at[1]),
    ]
    late = [
        pltpu.make_async_copy(own, passages.at[pl.ds(0, OWN)], sems.at[2]),
        pltpu.make_async_copy(sib, passages.at[pl.ds(OWN, OWN)], sems.at[3]),
    ]
    for copy in copies:
        copy.start()
    lines = [tiles[k, PIECES * ROWS : LINES, :].astype(F32) for k in range(X)]
    pos_name, pos_rest, names = [
        jnp.concatenate([line[i : i + 1] for line in lines], axis=0).astype(jnp.int32) for i in range(3)
    ]
    local = names - x * CHIP_BLOCKS
    turned = local + BLOCKS * c
    turned = jnp.where(turned >= CHIP_BLOCKS, turned - CHIP_BLOCKS, turned)
    slot = jnp.where((local >= 0) & (local < CHIP_BLOCKS), turned, -1)
    lane = lax.broadcasted_iota(jnp.int32, (X, ROWS), 1)
    pos_slot = jnp.full((X, ROWS), -1, jnp.int32)
    for n in range(NAMES):
        of_name = jnp.max(jnp.where(lane == n, slot, -1), axis=1, keepdims=True)
        pos_slot = jnp.where(pos_name == n, of_name, pos_slot)
    pos = flat(jnp.where(pos_slot >= 0, pos_slot * ROWS + pos_rest, -1))
    pos_row[...] = pos

    for k in range(X):
        for j in range(PIECES):
            rows[pl.ds(k * ROWS, ROWS), j * LANES : (j + 1) * LANES] = tiles[k, j * ROWS : (j + 1) * ROWS, :]
    project(rows[...], weight, proj, q_r, q_emb, X * ROWS)
    for copy in copies:
        copy.wait()
    mine = pl.ds(pl.multiple_of(x * ROWS, ROWS), ROWS)
    kept = [
        pltpu.make_async_copy(q_emb.at[mine], emb_mine, sems.at[4]),
        pltpu.make_async_copy(q_r.at[mine], r_mine, sems.at[5]),
    ]
    for copy in late + kept:
        copy.start()
    line = lax.broadcasted_iota(jnp.int32, (ROWS, X * ROWS), 0)
    total = jnp.zeros((1, X * ROWS), F32)
    picked = jnp.zeros((1, X * ROWS), F32)
    for h in range(C):
        half = matmul_nt(p_emb[pl.ds(h * OWN, OWN), :], q_emb[...])
        for i in range(BLOCKS):
            b = h * BLOCKS + i
            named = jnp.max(jnp.where(slot == b, 1, 0), axis=1, keepdims=True)
            named = flat(jnp.broadcast_to(named, (X, ROWS)))
            scores = half[i * ROWS : (i + 1) * ROWS] * score_scale
            value = jnp.where(named > 0, jnp.exp(scores), 0.0)
            exponent[pl.ds(b * ROWS, ROWS), :] = value
            total = total + jnp.sum(value, axis=0, keepdims=True)
            picked = picked + jnp.sum(jnp.where(line == pos - b * ROWS, scores, 0.0), axis=0, keepdims=True)
    send[...] = jnp.zeros(send.shape, F32)
    for k in range(X):
        lanes = slice(k * ROWS, (k + 1) * ROWS)
        for d in range(X):
            send[d, k : k + 1, :] = total[:, lanes]
        send[k, X : X + 1, :] = picked[:, lanes]
    for copy in late + kept:
        copy.wait()


def score_side(place, tiles, weight, emb_own, emb_sib, own, sib):
    queries = X * ROWS
    passages = CHIP_BLOCKS * ROWS
    return call(
        score_kernel, "score_side",
        (
            shape((queries, WIDTH), BF16),
            shape((queries, 1), F32),
            shape((passages, queries), F32),
            shape((X, 8, ROWS), F32),
            shape((1, queries), jnp.int32),
            shape((passages, WIDTH), BF16),
            shape((queries, WIDTH), BF16),
            shape((passages, WIDTH), BF16),
            pltpu.HBM((ROWS, WIDTH), BF16),
            pltpu.HBM((ROWS, 1), F32),
        ),
        [SMEM] + [VMEM] * 2 + [HBM] * 4,
        (VMEM,) * 8 + (HBM,) * 2,
        [
            pltpu.VMEM((queries, WIDTH), F32),
            pltpu.SemaphoreType.DMA((6,)),
        ],
        SCORE, 2_000_000_000, 8_000_000,
        place, tiles, weight, *in_hbm(emb_own, emb_sib, own, sib),
    )


def grad_kernel(
    place, recv, pos_row, exponent, q_r, r_own, r_sib, q_emb, p_emb, q_rows, passages,
    losses, g0, g1, g2, g3, p_grad_own, p_grad_sib, backs_here, w_there,
    dscore, q_grad, p_grad, backs,
):
    x, c = place[0], place[1]
    queries = X * ROWS
    total = recv[0] + recv[1] + recv[2] + recv[3]
    mine = jnp.zeros((1, ROWS), F32)
    for k in range(X):
        mine = mine + jnp.where(x == k, total[k : k + 1], 0.0)
    losses[...] = jnp.log(mine) - total[X : X + 1]
    inverse = 1.0 / flat(total)
    pos = pos_row[...]
    line = lax.broadcasted_iota(jnp.int32, (ROWS, queries), 0)
    for b in range(CHIP_BLOCKS):
        block = pl.ds(b * ROWS, ROWS)
        target = jnp.where(line == pos - b * ROWS, 1.0, 0.0)
        dscore[block, :] = (exponent[block, :] * inverse - target).astype(BF16)

    def keep(rows, emb, r, grad):
        value = back_of(emb, r * score_scale, grad).astype(BF16)
        low, high = value[:, :HALF], value[:, HALF:]
        backs[0, rows, :] = jnp.where(c == 0, low, high)
        backs[1, rows, :] = jnp.where(c == 0, high, low)

    for j in range(WIDTH // HALF):
        cols = pl.ds(j * HALF, HALF)
        q_grad[:, cols] = matmul_tn(dscore[...], p_emb[:, cols])
    for j in range(WIDTH // HALF):
        cols = pl.ds(j * HALF, HALF)
        p_grad[:, cols] = matmul(dscore[...], q_emb[:, cols])
    for k in range(X):
        rows = pl.ds(k * ROWS, ROWS)
        keep(rows, q_emb[rows, :], q_r[rows, :], q_grad[rows, :])
    for k, out in enumerate((g0, g1, g2, g3)):
        rows = pl.ds(pl.multiple_of(lax.rem(x + k, X) * ROWS, ROWS), ROWS)
        out[...] = q_grad[rows, :].astype(out.dtype)
    for b in range(CHIP_BLOCKS):
        rows = pl.ds(b * ROWS, ROWS)
        first = b < BLOCKS
        near = pl.ds((b % BLOCKS) * ROWS, ROWS)
        grad = p_grad[rows, :]
        (p_grad_own if first else p_grad_sib)[near, :] = grad.astype(BF16)
        r = (r_own if first else r_sib)[near, :]
        keep(pl.ds(queries + b * ROWS, ROWS), p_emb[rows, :], r, grad)
    weight_terms(q_rows, passages, backs.at[1], w_there)
    backs_here[...] = backs[0]


def weight_terms(q_rows, passages, backs, out):
    for j in range(WIDTH // HALF):
        cols = pl.ds(j * HALF, HALF)
        hidden = jnp.concatenate([q_rows[:, cols], passages[:, cols]], axis=0)
        out[cols, :] = matmul_tn(hidden, backs[...]).astype(out.dtype)


def grad_side(*args):
    queries = X * ROWS
    passages = CHIP_BLOCKS * ROWS
    tile = shape((ROWS, WIDTH), BF16)
    return call(
        grad_kernel, "grad_side",
        (
            shape((1, ROWS), F32),
            tile, tile, tile, tile,
            shape((OWN, WIDTH), BF16),
            shape((OWN, WIDTH), BF16),
            shape((queries + passages, HALF), BF16),
            shape((WIDTH, HALF), BF16),
        ),
        [SMEM] + [VMEM] * 10,
        (VMEM,) * 9,
        [
            pltpu.VMEM((passages, queries), BF16),
            pltpu.VMEM((queries, WIDTH), F32),
            pltpu.VMEM((passages, WIDTH), F32),
            pltpu.VMEM((C, queries + passages, HALF), BF16),
        ],
        GRAD, 3_000_000_000, 14_000_000,
        *args,
    )


def weight_kernel(backs, q_rows, passages, out):
    weight_terms(q_rows, passages, backs, out)


def weight_here(backs, q_rows, passages):
    return call(
        weight_kernel, "weight_here",
        shape((WIDTH, HALF), F32),
        [VMEM] * 3,
        VMEM,
        [],
        24, 1_350_000_000, 6_000_000,
        backs, q_rows, passages,
    )


def spread_kernel(here, there, out, held, sems):
    own_rows = WIDTH // (Z * Y)
    lanes = HALF // X
    copies = []
    for y in range(Y):
        for h in range(2):
            for z in range(h * Z // 2, (h + 1) * Z // 2):
                rows = pl.ds((z * Y + y) * own_rows, own_rows)
                value = (here[rows, :] + there[rows, :].astype(F32)).astype(BF16)
                for x in range(X):
                    held[y * X + x, z] = value[:, x * lanes : (x + 1) * lanes]
            part = (pl.ds(y * X, X), pl.ds(h * Z // 2, Z // 2))
            copies.append(pltpu.make_async_copy(held.at[part], out.at[part], sems.at[2 * y + h]))
            copies[-1].start()
    for copy in copies:
        copy.wait()


def spread(here, there):
    dims = (Y * X, Z, WIDTH // (Z * Y), HALF // X)
    return call(
        spread_kernel, "spread",
        pltpu.HBM(dims, BF16),
        [VMEM, VMEM],
        HBM,
        [pltpu.VMEM(dims, BF16), pltpu.SemaphoreType.DMA((2 * Y,))],
        16, 500_000, 4_000_000,
        here, there,
    )


def sum_kernel(pieces, out):
    total = pieces[0].astype(F32)
    for k in range(1, pieces.shape[0]):
        total = total + pieces[k].astype(F32)
    out[...] = total.astype(BF16)


def sum_pieces(pieces):
    return call(
        sum_kernel, "sum_pieces", shape(pieces.shape[1:], BF16), [VMEM], VMEM, [], 8, 500_000, 1_000_000, pieces
    )


def last_sum_kernel(pieces, out):
    total = pieces[0].astype(F32)
    for k in range(1, Z):
        total = total + pieces[k].astype(F32)
    total = total * (1.0 / (Z * Y * X * C))
    for d in range(X * C):
        out[d] = total


def last_sum(pieces):
    dims = (X * C,) + pieces.shape[1:]
    return call(
        last_sum_kernel, "last_sum", shape(dims, F32), [VMEM], VMEM, [], 8, 50_000, 100_000, pieces
    )


def lay_kernel(pieces, out):
    lanes = HALF // X
    for x in range(X):
        for c in range(C):
            out[:, c * HALF + x * lanes : c * HALF + (x + 1) * lanes] = pieces[x * C + c]


def lay(pieces):
    dims = (WIDTH // (Z * Y), WIDTH)
    return call(lay_kernel, "lay", shape(dims, F32), [VMEM], VMEM, [], 8, 0, 200_000, pieces)


def hidden_kernel(*refs):
    *terms, emb, r, weight, out = refs
    grad = terms[0][...].astype(F32)
    for term in terms[1:]:
        grad = grad + term[...].astype(F32)
    back = back_of(emb[...], r[...] * score_scale, grad).astype(BF16)
    for j in range(WIDTH // PART):
        cols = pl.ds(j * PART, PART)
        out[:, cols] = matmul_nt(back, weight[cols, :]).astype(BF16)


def hidden_grad(terms, emb, r, weight, far=False):
    rows = emb.shape[0]
    return call(
        hidden_kernel, "hidden_grad",
        shape((rows, WIDTH), BF16),
        [VMEM] * (len(terms) + 3),
        VMEM,
        [],
        24, 2 * rows * WIDTH * WIDTH, 2_000_000 + rows * 10_000,
        *(in_hbm(terms[0]) if far else terms[:1]), *terms[1:], *in_hbm(emb, r), weight,
    )


def body(queries, passages, weight, pairs, positive):
    x = lax.axis_index("x")
    c = lax.axis_index("c")
    place = jnp.stack([x, c]).astype(jnp.int32)

    packed = pack(queries, positive, pairs)
    tiles = exchange(packed, "x")
    passages, weight, _ = lax.optimization_barrier((passages, weight, packed))
    emb_own, r_own = passage_side(passages, weight)
    outgoing, _ = lax.optimization_barrier((passages, emb_own))
    sibling = lax.ppermute(outgoing, "c", SWAP)
    emb_sib, r_sib = passage_side(sibling, weight)

    q_emb, q_r, exponent, send, pos_row, p_emb, q_rows, hidden, emb_mine, r_mine = score_side(
        place, tiles, weight, emb_own, emb_sib, passages, sibling
    )
    recv = exchange(send, "x")
    losses, g0, g1, g2, g3, p_grad, p_grad_sib, backs, w_there = grad_side(
        place, recv, pos_row, exponent, q_r, r_own, r_sib, q_emb, p_emb, q_rows, hidden
    )

    w_there = lax.ppermute(w_there, "c", SWAP)
    w = spread(weight_here(backs, q_rows, hidden), w_there)
    (p_grad_sib, g1, g2, g3), w = lax.optimization_barrier(((p_grad_sib, g1, g2, g3), w))
    g2 = lax.ppermute(g2, "x", shift(X - 2))
    g1 = lax.ppermute(g1, "x", shift(X - 1))
    g3 = lax.ppermute(g3, "x", shift(X - 3))
    query_grad = hidden_grad((g0, g1, g2, g3), emb_mine, r_mine, weight)
    p_grad_sib = lax.ppermute(p_grad_sib, "c", SWAP)
    passage_grad = hidden_grad((p_grad, p_grad_sib), emb_own, r_own, weight, far=True)

    w = sum_pieces(exchange(w, ("y", "x")))
    w, passage_grad = lax.optimization_barrier((w, passage_grad))
    w = exchange(w, "z")
    w, query_grad = lax.optimization_barrier((w, query_grad))
    w = last_sum(w)
    weight_grad = lay(exchange(w, ("x", "c")))
    return losses.reshape(ROWS), query_grad, passage_grad, weight_grad


def solution(mesh):
    torus = Mesh(mesh.devices.reshape(Z, Y, X, C), ("z", "y", "x", "c"))
    every = ("z", "y", "x", "c")
    return jax.shard_map(
        body,
        mesh=torus,
        in_specs=(P(every, None), P(every, None), P(), P(every, None), P(every)),
        out_specs=(P(every), P(every, None), P(every, None), P(("z", "y"), None)),
        check_vma=False,
    )
```

```python
import jax
import jax.numpy as jnp
from jax import lax
from jax.experimental import pallas as pl
from jax.experimental.pallas import tpu as pltpu
from jax.sharding import Mesh, PartitionSpec as P

score_scale = 50.0
epsilon = 1e-06

X, C, Y, Z = 4, 2, 4, 16
SWAP = ((0, 1), (1, 0))
ROWS = 128
WIDTH = 1024
OWN = 384
BLOCKS = OWN // ROWS
CHIP_BLOCKS = BLOCKS * C
NAMES = 8
LANES = 128
PIECES = WIDTH // LANES
EXTRA = 16
LINES = PIECES * ROWS + EXTRA
HALF = WIDTH // C
PART = 512
HBM = pl.BlockSpec(memory_space=pltpu.HBM)
VMEM = pl.BlockSpec(memory_space=pltpu.VMEM)
SMEM = pl.BlockSpec(memory_space=pltpu.SMEM)
F32, BF16 = jnp.float32, jnp.bfloat16
SCORE = 24
GRAD = 32


def shift(k):
    return tuple(((i + k) % X, i) for i in range(X))


def exchange(value, axis):
    return lax.all_to_all(value, axis, split_axis=0, concat_axis=0, tiled=True)


def matmul(a, b):
    return jnp.dot(a, b, preferred_element_type=F32)


def matmul_tn(a, b):
    return lax.dot_general(a, b, (((0,), (0,)), ((), ())), preferred_element_type=F32)


def matmul_nt(a, b):
    return lax.dot_general(a, b, (((1,), (1,)), ((), ())), preferred_element_type=F32)


def back_of(emb, r, grad):
    emb = emb.astype(F32)
    inner = jnp.sum(emb * grad, axis=-1, keepdims=True)
    return r * (grad - inner * emb)


def params(mib):
    return pltpu.CompilerParams(vmem_limit_bytes=mib << 20)


def in_hbm(*values):
    return [pltpu.with_memory_space_constraint(value, pltpu.HBM) for value in values]


def shape(dims, dtype):
    return jax.ShapeDtypeStruct(dims, dtype)


def call(kernel, name, out_shape, in_specs, out_specs, scratch, mib, flops, moved, *args):
    return pl.pallas_call(
        kernel,
        name=name,
        out_shape=out_shape,
        in_specs=in_specs,
        out_specs=out_specs,
        scratch_shapes=scratch,
        compiler_params=params(mib),
        cost_estimate=pl.CostEstimate(flops=flops, bytes_accessed=moved, transcendentals=0),
    )(*args)


def pack_kernel(queries, positive, pairs, out, pos, names, rows, wide, packed, sems):
    inner = [
        pltpu.make_async_copy(queries, rows, sems.at[X]),
        pltpu.make_async_copy(positive, pos, sems.at[X + 1]),
        pltpu.make_async_copy(pairs, names, sems.at[X + 2]),
    ]
    for copy in inner:
        copy.start()
    wide[...] = jnp.full(wide.shape, 255.0, F32)
    inner[1].wait()
    inner[2].wait()
    index = pos[...]
    wide[0:1, :] = (index >> 7).astype(F32)
    wide[1:2, :] = (index & 127).astype(F32)
    wide[2:3, 0:NAMES] = names[...].astype(F32)
    packed[pl.ds(PIECES * ROWS, EXTRA), :] = wide[...].astype(BF16)
    inner[0].wait()
    for j in range(PIECES):
        packed[pl.ds(j * ROWS, ROWS), :] = rows[:, j * LANES : (j + 1) * LANES]
    copies = [pltpu.make_async_copy(packed, out.at[d], sems.at[d]) for d in range(X)]
    for copy in copies:
        copy.start()
    for copy in copies:
        copy.wait()


def pack(queries, positive, pairs):
    return call(
        pack_kernel, "pack",
        pltpu.HBM((X, LINES, LANES), BF16),
        [HBM, HBM, HBM],
        HBM,
        [
            pltpu.VMEM((1, ROWS), jnp.int32),
            pltpu.VMEM((1, NAMES), jnp.int32),
            pltpu.VMEM((ROWS, WIDTH), BF16),
            pltpu.VMEM((EXTRA, LANES), F32),
            pltpu.VMEM((LINES, LANES), BF16),
            pltpu.SemaphoreType.DMA((X + 3,)),
        ],
        4, 0, 1_400_000,
        *in_hbm(queries, positive.reshape(1, ROWS), pairs),
    )


def project(source, weight, proj, r_out, emb, rows):
    for j in range(WIDTH // PART):
        cols = pl.ds(j * PART, PART)
        proj[:, cols] = matmul(source, weight[:, cols])
    for i in range(rows // ROWS):
        here = pl.ds(i * ROWS, ROWS)
        value = proj[here, :]
        r = lax.rsqrt(jnp.sum(value * value, axis=1, keepdims=True) + epsilon)
        r_out[here, :] = r
        emb[here, :] = (value * r).astype(BF16)


def passage_kernel(passages, weight, emb, r_out, proj):
    project(passages[...], weight, proj, r_out, emb, OWN)


def passage_side(passages, weight):
    return call(
        passage_kernel, "passage_side",
        (pltpu.HBM((OWN, WIDTH), BF16), pltpu.HBM((OWN, 1), F32)),
        [VMEM, VMEM],
        (VMEM, VMEM),
        [pltpu.VMEM((OWN, WIDTH), F32)],
        16, 1_000, 1_000,
        passages, weight,
    )


def flat(value):
    return jnp.concatenate([value[k : k + 1] for k in range(X)], axis=1)


def score_kernel(
    place, tiles, weight, emb_own, emb_sib, own, sib,
    q_emb, q_r, exponent, send, pos_row, p_emb, rows, passages, emb_mine, r_mine,
    proj, sems,
):
    x, c = place[0], place[1]
    copies = [
        pltpu.make_async_copy(emb_own, p_emb.at[pl.ds(0, OWN)], sems.at[0]),
        pltpu.make_async_copy(emb_sib, p_emb.at[pl.ds(OWN, OWN)], sems.at[1]),
    ]
    late = [
        pltpu.make_async_copy(own, passages.at[pl.ds(0, OWN)], sems.at[2]),
        pltpu.make_async_copy(sib, passages.at[pl.ds(OWN, OWN)], sems.at[3]),
    ]
    for copy in copies + late:
        copy.start()
    lines = [tiles[k, PIECES * ROWS : LINES, :].astype(F32) for k in range(X)]
    pos_name, pos_rest, names = [
        jnp.concatenate([line[i : i + 1] for line in lines], axis=0).astype(jnp.int32) for i in range(3)
    ]
    local = names - x * CHIP_BLOCKS
    turned = local + BLOCKS * c
    turned = jnp.where(turned >= CHIP_BLOCKS, turned - CHIP_BLOCKS, turned)
    slot = jnp.where((local >= 0) & (local < CHIP_BLOCKS), turned, -1)
    lane = lax.broadcasted_iota(jnp.int32, (X, ROWS), 1)
    pos_slot = jnp.full((X, ROWS), -1, jnp.int32)
    for n in range(NAMES):
        of_name = jnp.max(jnp.where(lane == n, slot, -1), axis=1, keepdims=True)
        pos_slot = jnp.where(pos_name == n, of_name, pos_slot)
    pos = flat(jnp.where(pos_slot >= 0, pos_slot * ROWS + pos_rest, -1))
    pos_row[...] = pos

    for k in range(X):
        for j in range(PIECES):
            rows[pl.ds(k * ROWS, ROWS), j * LANES : (j + 1) * LANES] = tiles[k, j * ROWS : (j + 1) * ROWS, :]
    project(rows[...], weight, proj, q_r, q_emb, X * ROWS)
    for copy in copies:
        copy.wait()
    mine = pl.ds(pl.multiple_of(x * ROWS, ROWS), ROWS)
    kept = [
        pltpu.make_async_copy(q_emb.at[mine], emb_mine, sems.at[4]),
        pltpu.make_async_copy(q_r.at[mine], r_mine, sems.at[5]),
    ]
    for copy in kept:
        copy.start()
    line = lax.broadcasted_iota(jnp.int32, (ROWS, X * ROWS), 0)
    total = jnp.zeros((1, X * ROWS), F32)
    picked = jnp.zeros((1, X * ROWS), F32)
    for h in range(C):
        half = matmul_nt(p_emb[pl.ds(h * OWN, OWN), :], q_emb[...])
        for i in range(BLOCKS):
            b = h * BLOCKS + i
            named = jnp.max(jnp.where(slot == b, 1, 0), axis=1, keepdims=True)
            named = flat(jnp.broadcast_to(named, (X, ROWS)))
            scores = half[i * ROWS : (i + 1) * ROWS] * score_scale
            value = jnp.where(named > 0, jnp.exp(scores), 0.0)
            exponent[pl.ds(b * ROWS, ROWS), :] = value
            total = total + jnp.sum(value, axis=0, keepdims=True)
            picked = picked + jnp.sum(jnp.where(line == pos - b * ROWS, scores, 0.0), axis=0, keepdims=True)
    send[...] = jnp.zeros(send.shape, F32)
    for k in range(X):
        lanes = slice(k * ROWS, (k + 1) * ROWS)
        for d in range(X):
            send[d, k : k + 1, :] = total[:, lanes]
        send[k, X : X + 1, :] = picked[:, lanes]
    for copy in late + kept:
        copy.wait()


def score_side(place, tiles, weight, emb_own, emb_sib, own, sib):
    queries = X * ROWS
    passages = CHIP_BLOCKS * ROWS
    return call(
        score_kernel, "score_side",
        (
            shape((queries, WIDTH), BF16),
            shape((queries, 1), F32),
            shape((passages, queries), F32),
            shape((X, 8, ROWS), F32),
            shape((1, queries), jnp.int32),
            shape((passages, WIDTH), BF16),
            shape((queries, WIDTH), BF16),
            shape((passages, WIDTH), BF16),
            pltpu.HBM((ROWS, WIDTH), BF16),
            pltpu.HBM((ROWS, 1), F32),
        ),
        [SMEM] + [VMEM] * 2 + [HBM] * 4,
        (VMEM,) * 8 + (HBM,) * 2,
        [
            pltpu.VMEM((queries, WIDTH), F32),
            pltpu.SemaphoreType.DMA((6,)),
        ],
        SCORE, 2_000_000_000, 8_000_000,
        place, tiles, weight, *in_hbm(emb_own, emb_sib, own, sib),
    )


def grad_kernel(
    place, recv, pos_row, exponent, q_r, r_own, r_sib, q_emb, p_emb, q_rows, passages,
    losses, g0, g1, g2, g3, p_grad_own, p_grad_sib, backs_here, w_there,
    dscore, q_grad, p_grad, backs,
):
    x, c = place[0], place[1]
    queries = X * ROWS
    total = recv[0] + recv[1] + recv[2] + recv[3]
    mine = jnp.zeros((1, ROWS), F32)
    for k in range(X):
        mine = mine + jnp.where(x == k, total[k : k + 1], 0.0)
    losses[...] = jnp.log(mine) - total[X : X + 1]
    inverse = 1.0 / flat(total)
    pos = pos_row[...]
    line = lax.broadcasted_iota(jnp.int32, (ROWS, queries), 0)
    for b in range(CHIP_BLOCKS):
        block = pl.ds(b * ROWS, ROWS)
        target = jnp.where(line == pos - b * ROWS, 1.0, 0.0)
        dscore[block, :] = (exponent[block, :] * inverse - target).astype(BF16)

    def keep(rows, emb, r, grad):
        value = back_of(emb, r * score_scale, grad).astype(BF16)
        low, high = value[:, :HALF], value[:, HALF:]
        backs[0, rows, :] = jnp.where(c == 0, low, high)
        backs[1, rows, :] = jnp.where(c == 0, high, low)

    for j in range(WIDTH // HALF):
        cols = pl.ds(j * HALF, HALF)
        q_grad[:, cols] = matmul_tn(dscore[...], p_emb[:, cols])
    for j in range(WIDTH // HALF):
        cols = pl.ds(j * HALF, HALF)
        p_grad[:, cols] = matmul(dscore[...], q_emb[:, cols])
    for k in range(X):
        rows = pl.ds(k * ROWS, ROWS)
        keep(rows, q_emb[rows, :], q_r[rows, :], q_grad[rows, :])
    for k, out in enumerate((g0, g1, g2, g3)):
        rows = pl.ds(pl.multiple_of(lax.rem(x + k, X) * ROWS, ROWS), ROWS)
        out[...] = q_grad[rows, :].astype(out.dtype)
    for b in range(CHIP_BLOCKS):
        rows = pl.ds(b * ROWS, ROWS)
        first = b < BLOCKS
        near = pl.ds((b % BLOCKS) * ROWS, ROWS)
        grad = p_grad[rows, :]
        (p_grad_own if first else p_grad_sib)[near, :] = grad.astype(BF16)
        r = (r_own if first else r_sib)[near, :]
        keep(pl.ds(queries + b * ROWS, ROWS), p_emb[rows, :], r, grad)
    weight_terms(q_rows, passages, backs.at[1], w_there)
    backs_here[...] = backs[0]


def weight_terms(q_rows, passages, backs, out):
    for j in range(WIDTH // HALF):
        cols = pl.ds(j * HALF, HALF)
        hidden = jnp.concatenate([q_rows[:, cols], passages[:, cols]], axis=0)
        out[cols, :] = matmul_tn(hidden, backs[...]).astype(out.dtype)


def grad_side(*args):
    queries = X * ROWS
    passages = CHIP_BLOCKS * ROWS
    tile = shape((ROWS, WIDTH), BF16)
    return call(
        grad_kernel, "grad_side",
        (
            shape((1, ROWS), F32),
            tile, tile, tile, tile,
            shape((OWN, WIDTH), BF16),
            shape((OWN, WIDTH), BF16),
            shape((queries + passages, HALF), BF16),
            shape((WIDTH, HALF), BF16),
        ),
        [SMEM] + [VMEM] * 10,
        (VMEM,) * 9,
        [
            pltpu.VMEM((passages, queries), BF16),
            pltpu.VMEM((queries, WIDTH), F32),
            pltpu.VMEM((passages, WIDTH), F32),
            pltpu.VMEM((C, queries + passages, HALF), BF16),
        ],
        GRAD, 3_000_000_000, 14_000_000,
        *args,
    )


def weight_kernel(backs, q_rows, passages, out):
    weight_terms(q_rows, passages, backs, out)


def weight_here(backs, q_rows, passages):
    return call(
        weight_kernel, "weight_here",
        shape((WIDTH, HALF), F32),
        [VMEM] * 3,
        VMEM,
        [],
        24, 1_350_000_000, 6_000_000,
        backs, q_rows, passages,
    )


def spread_kernel(here, there, out, held, sems):
    own_rows = WIDTH // (Z * Y)
    lanes = HALF // X
    copies = []
    for y in range(Y):
        for h in range(2):
            for z in range(h * Z // 2, (h + 1) * Z // 2):
                rows = pl.ds((z * Y + y) * own_rows, own_rows)
                value = (here[rows, :] + there[rows, :].astype(F32)).astype(BF16)
                for x in range(X):
                    held[y * X + x, z] = value[:, x * lanes : (x + 1) * lanes]
            part = (pl.ds(y * X, X), pl.ds(h * Z // 2, Z // 2))
            copies.append(pltpu.make_async_copy(held.at[part], out.at[part], sems.at[2 * y + h]))
            copies[-1].start()
    for copy in copies:
        copy.wait()


def spread(here, there):
    dims = (Y * X, Z, WIDTH // (Z * Y), HALF // X)
    return call(
        spread_kernel, "spread",
        pltpu.HBM(dims, BF16),
        [VMEM, VMEM],
        HBM,
        [pltpu.VMEM(dims, BF16), pltpu.SemaphoreType.DMA((2 * Y,))],
        16, 500_000, 4_000_000,
        here, there,
    )


def sum_kernel(pieces, out):
    total = pieces[0].astype(F32)
    for k in range(1, pieces.shape[0]):
        total = total + pieces[k].astype(F32)
    out[...] = total.astype(BF16)


def sum_pieces(pieces):
    return call(
        sum_kernel, "sum_pieces", shape(pieces.shape[1:], BF16), [VMEM], VMEM, [], 8, 500_000, 1_000_000, pieces
    )


def last_sum_kernel(pieces, out):
    total = pieces[0].astype(F32)
    for k in range(1, Z):
        total = total + pieces[k].astype(F32)
    total = total * (1.0 / (Z * Y * X * C))
    for d in range(X * C):
        out[d] = total


def last_sum(pieces):
    dims = (X * C,) + pieces.shape[1:]
    return call(
        last_sum_kernel, "last_sum", shape(dims, F32), [VMEM], VMEM, [], 8, 50_000, 100_000, pieces
    )


def lay_kernel(pieces, out):
    lanes = HALF // X
    for x in range(X):
        for c in range(C):
            out[:, c * HALF + x * lanes : c * HALF + (x + 1) * lanes] = pieces[x * C + c]


def lay(pieces):
    dims = (WIDTH // (Z * Y), WIDTH)
    return call(lay_kernel, "lay", shape(dims, F32), [VMEM], VMEM, [], 8, 0, 200_000, pieces)


def hidden_kernel(*refs):
    *terms, emb, r, weight, out = refs
    grad = terms[0][...].astype(F32)
    for term in terms[1:]:
        grad = grad + term[...].astype(F32)
    back = back_of(emb[...], r[...] * score_scale, grad).astype(BF16)
    for j in range(WIDTH // PART):
        cols = pl.ds(j * PART, PART)
        out[:, cols] = matmul_nt(back, weight[cols, :]).astype(BF16)


def hidden_grad(terms, emb, r, weight, far=False):
    rows = emb.shape[0]
    block = pl.BlockSpec((ROWS, WIDTH), lambda i: (i, 0))
    return pl.pallas_call(
        hidden_kernel,
        name="hidden_grad",
        grid=(rows // ROWS,),
        out_shape=shape((rows, WIDTH), BF16),
        in_specs=[block] * (len(terms) + 1) + [pl.BlockSpec((ROWS, 1), lambda i: (i, 0)), VMEM],
        out_specs=block,
        compiler_params=params(24),
        cost_estimate=pl.CostEstimate(
            flops=2 * rows * WIDTH * WIDTH, bytes_accessed=2_000_000 + rows * 10_000, transcendentals=0
        ),
    )(*(in_hbm(terms[0]) if far else terms[:1]), *terms[1:], *in_hbm(emb, r), weight)


def body(queries, passages, weight, pairs, positive):
    x = lax.axis_index("x")
    c = lax.axis_index("c")
    place = jnp.stack([x, c]).astype(jnp.int32)

    packed = pack(queries, positive, pairs)
    tiles = exchange(packed, "x")
    passages, weight, _ = lax.optimization_barrier((passages, weight, packed))
    emb_own, r_own = passage_side(passages, weight)
    outgoing, _ = lax.optimization_barrier((passages, emb_own))
    sibling = lax.ppermute(outgoing, "c", SWAP)
    emb_sib, r_sib = passage_side(sibling, weight)

    q_emb, q_r, exponent, send, pos_row, p_emb, q_rows, hidden, emb_mine, r_mine = score_side(
        place, tiles, weight, emb_own, emb_sib, passages, sibling
    )
    recv = exchange(send, "x")
    losses, g0, g1, g2, g3, p_grad, p_grad_sib, backs, w_there = grad_side(
        place, recv, pos_row, exponent, q_r, r_own, r_sib, q_emb, p_emb, q_rows, hidden
    )

    w_there = lax.ppermute(w_there, "c", SWAP)
    w = spread(weight_here(backs, q_rows, hidden), w_there)
    (p_grad_sib, g1, g2, g3), w = lax.optimization_barrier(((p_grad_sib, g1, g2, g3), w))
    g2 = lax.ppermute(g2, "x", shift(X - 2))
    g1 = lax.ppermute(g1, "x", shift(X - 1))
    g3 = lax.ppermute(g3, "x", shift(X - 3))
    query_grad = hidden_grad((g0, g1, g2, g3), emb_mine, r_mine, weight)
    p_grad_sib = lax.ppermute(p_grad_sib, "c", SWAP)
    passage_grad = hidden_grad((p_grad, p_grad_sib), emb_own, r_own, weight, far=True)

    w = sum_pieces(exchange(w, ("y", "x")))
    w, passage_grad = lax.optimization_barrier((w, passage_grad))
    w = exchange(w, "z")
    w, query_grad = lax.optimization_barrier((w, query_grad))
    w = last_sum(w)
    weight_grad = lay(exchange(w, ("x", "c")))
    return losses.reshape(ROWS), query_grad, passage_grad, weight_grad


def solution(mesh):
    torus = Mesh(mesh.devices.reshape(Z, Y, X, C), ("z", "y", "x", "c"))
    every = ("z", "y", "x", "c")
    return jax.shard_map(
        body,
        mesh=torus,
        in_specs=(P(every, None), P(every, None), P(), P(every, None), P(every)),
        out_specs=(P(every), P(every, None), P(every, None), P(("z", "y"), None)),
        check_vma=False,
    )
```

```python
import jax
import jax.numpy as jnp
from jax import lax
from jax.experimental import pallas as pl
from jax.experimental.pallas import tpu as pltpu
from jax.sharding import Mesh, PartitionSpec as P

score_scale = 50.0
epsilon = 1e-06

X, C, Y, Z = 4, 2, 4, 16
SWAP = ((0, 1), (1, 0))
ROWS = 128
WIDTH = 1024
OWN = 384
BLOCKS = OWN // ROWS
CHIP_BLOCKS = BLOCKS * C
NAMES = 8
LANES = 128
PIECES = WIDTH // LANES
EXTRA = 16
LINES = PIECES * ROWS + EXTRA
HALF = WIDTH // C
PART = 512
HBM = pl.BlockSpec(memory_space=pltpu.HBM)
VMEM = pl.BlockSpec(memory_space=pltpu.VMEM)
SMEM = pl.BlockSpec(memory_space=pltpu.SMEM)
F32, BF16 = jnp.float32, jnp.bfloat16
SCORE = 24
GRAD = 32


def shift(k):
    return tuple(((i + k) % X, i) for i in range(X))


def exchange(value, axis):
    return lax.all_to_all(value, axis, split_axis=0, concat_axis=0, tiled=True)


def matmul(a, b):
    return jnp.dot(a, b, preferred_element_type=F32)


def matmul_tn(a, b):
    return lax.dot_general(a, b, (((0,), (0,)), ((), ())), preferred_element_type=F32)


def matmul_nt(a, b):
    return lax.dot_general(a, b, (((1,), (1,)), ((), ())), preferred_element_type=F32)


def back_of(emb, r, grad):
    emb = emb.astype(F32)
    inner = jnp.sum(emb * grad, axis=-1, keepdims=True)
    return r * (grad - inner * emb)


def params(mib):
    return pltpu.CompilerParams(vmem_limit_bytes=mib << 20)


def in_hbm(*values):
    return [pltpu.with_memory_space_constraint(value, pltpu.HBM) for value in values]


def shape(dims, dtype):
    return jax.ShapeDtypeStruct(dims, dtype)


def call(kernel, name, out_shape, in_specs, out_specs, scratch, mib, flops, moved, *args):
    return pl.pallas_call(
        kernel,
        name=name,
        out_shape=out_shape,
        in_specs=in_specs,
        out_specs=out_specs,
        scratch_shapes=scratch,
        compiler_params=params(mib),
        cost_estimate=pl.CostEstimate(flops=flops, bytes_accessed=moved, transcendentals=0),
    )(*args)


def pack_kernel(queries, positive, pairs, out, pos, names, rows, wide, packed, sems):
    inner = [
        pltpu.make_async_copy(queries, rows, sems.at[X]),
        pltpu.make_async_copy(positive, pos, sems.at[X + 1]),
        pltpu.make_async_copy(pairs, names, sems.at[X + 2]),
    ]
    for copy in inner:
        copy.start()
    wide[...] = jnp.full(wide.shape, 255.0, F32)
    inner[1].wait()
    inner[2].wait()
    index = pos[...]
    wide[0:1, :] = (index >> 7).astype(F32)
    wide[1:2, :] = (index & 127).astype(F32)
    wide[2:3, 0:NAMES] = names[...].astype(F32)
    packed[pl.ds(PIECES * ROWS, EXTRA), :] = wide[...].astype(BF16)
    inner[0].wait()
    for j in range(PIECES):
        packed[pl.ds(j * ROWS, ROWS), :] = rows[:, j * LANES : (j + 1) * LANES]
    copies = [pltpu.make_async_copy(packed, out.at[d], sems.at[d]) for d in range(X)]
    for copy in copies:
        copy.start()
    for copy in copies:
        copy.wait()


def pack(queries, positive, pairs):
    return call(
        pack_kernel, "pack",
        pltpu.HBM((X, LINES, LANES), BF16),
        [HBM, HBM, HBM],
        HBM,
        [
            pltpu.VMEM((1, ROWS), jnp.int32),
            pltpu.VMEM((1, NAMES), jnp.int32),
            pltpu.VMEM((ROWS, WIDTH), BF16),
            pltpu.VMEM((EXTRA, LANES), F32),
            pltpu.VMEM((LINES, LANES), BF16),
            pltpu.SemaphoreType.DMA((X + 3,)),
        ],
        4, 0, 1_400_000,
        *in_hbm(queries, positive.reshape(1, ROWS), pairs),
    )


def project(source, weight, proj, r_out, emb, rows):
    for j in range(WIDTH // PART):
        cols = pl.ds(j * PART, PART)
        proj[:, cols] = matmul(source, weight[:, cols])
    for i in range(rows // ROWS):
        here = pl.ds(i * ROWS, ROWS)
        value = proj[here, :]
        r = lax.rsqrt(jnp.sum(value * value, axis=1, keepdims=True) + epsilon)
        r_out[here, :] = r
        emb[here, :] = (value * r).astype(BF16)


def passage_kernel(passages, weight, emb, r_out, proj):
    project(passages[...], weight, proj, r_out, emb, OWN)


def passage_side(passages, weight):
    return call(
        passage_kernel, "passage_side",
        (pltpu.HBM((OWN, WIDTH), BF16), pltpu.HBM((OWN, 1), F32)),
        [VMEM, VMEM],
        (VMEM, VMEM),
        [pltpu.VMEM((OWN, WIDTH), F32)],
        16, 1_000, 1_000,
        passages, weight,
    )


def flat(value):
    return jnp.concatenate([value[k : k + 1] for k in range(X)], axis=1)


def score_kernel(
    place, tiles, weight, emb_own, emb_sib, own, sib,
    q_emb, q_r, exponent, send, pos_row, p_emb, rows, passages, emb_mine, r_mine,
    proj, sems,
):
    x, c = place[0], place[1]
    copies = [
        pltpu.make_async_copy(emb_own, p_emb.at[pl.ds(0, OWN)], sems.at[0]),
        pltpu.make_async_copy(emb_sib, p_emb.at[pl.ds(OWN, OWN)], sems.at[1]),
    ]
    late = [
        pltpu.make_async_copy(own, passages.at[pl.ds(0, OWN)], sems.at[2]),
        pltpu.make_async_copy(sib, passages.at[pl.ds(OWN, OWN)], sems.at[3]),
    ]
    for copy in copies + late:
        copy.start()
    lines = [tiles[k, PIECES * ROWS : LINES, :].astype(F32) for k in range(X)]
    pos_name, pos_rest, names = [
        jnp.concatenate([line[i : i + 1] for line in lines], axis=0).astype(jnp.int32) for i in range(3)
    ]
    local = names - x * CHIP_BLOCKS
    turned = local + BLOCKS * c
    turned = jnp.where(turned >= CHIP_BLOCKS, turned - CHIP_BLOCKS, turned)
    slot = jnp.where((local >= 0) & (local < CHIP_BLOCKS), turned, -1)
    lane = lax.broadcasted_iota(jnp.int32, (X, ROWS), 1)
    pos_slot = jnp.full((X, ROWS), -1, jnp.int32)
    for n in range(NAMES):
        of_name = jnp.max(jnp.where(lane == n, slot, -1), axis=1, keepdims=True)
        pos_slot = jnp.where(pos_name == n, of_name, pos_slot)
    pos = flat(jnp.where(pos_slot >= 0, pos_slot * ROWS + pos_rest, -1))
    pos_row[...] = pos

    for k in range(X):
        for j in range(PIECES):
            rows[pl.ds(k * ROWS, ROWS), j * LANES : (j + 1) * LANES] = tiles[k, j * ROWS : (j + 1) * ROWS, :]
    project(rows[...], weight, proj, q_r, q_emb, X * ROWS)
    for copy in copies:
        copy.wait()
    mine = pl.ds(pl.multiple_of(x * ROWS, ROWS), ROWS)
    kept = [
        pltpu.make_async_copy(q_emb.at[mine], emb_mine, sems.at[4]),
        pltpu.make_async_copy(q_r.at[mine], r_mine, sems.at[5]),
    ]
    for copy in kept:
        copy.start()
    line = lax.broadcasted_iota(jnp.int32, (ROWS, X * ROWS), 0)
    total = jnp.zeros((1, X * ROWS), F32)
    picked = jnp.zeros((1, X * ROWS), F32)
    for h in range(C):
        half = matmul_nt(p_emb[pl.ds(h * OWN, OWN), :], q_emb[...])
        for i in range(BLOCKS):
            b = h * BLOCKS + i
            named = jnp.max(jnp.where(slot == b, 1, 0), axis=1, keepdims=True)
            named = flat(jnp.broadcast_to(named, (X, ROWS)))
            scores = half[i * ROWS : (i + 1) * ROWS] * score_scale
            value = jnp.where(named > 0, jnp.exp(scores), 0.0)
            exponent[pl.ds(b * ROWS, ROWS), :] = value
            total = total + jnp.sum(value, axis=0, keepdims=True)
            picked = picked + jnp.sum(jnp.where(line == pos - b * ROWS, scores, 0.0), axis=0, keepdims=True)
    send[...] = jnp.zeros(send.shape, F32)
    for k in range(X):
        lanes = slice(k * ROWS, (k + 1) * ROWS)
        for d in range(X):
            send[d, k : k + 1, :] = total[:, lanes]
        send[k, X : X + 1, :] = picked[:, lanes]
    for copy in late + kept:
        copy.wait()


def score_side(place, tiles, weight, emb_own, emb_sib, own, sib):
    queries = X * ROWS
    passages = CHIP_BLOCKS * ROWS
    return call(
        score_kernel, "score_side",
        (
            shape((queries, WIDTH), BF16),
            shape((queries, 1), F32),
            shape((passages, queries), F32),
            shape((X, 8, ROWS), F32),
            shape((1, queries), jnp.int32),
            shape((passages, WIDTH), BF16),
            shape((queries, WIDTH), BF16),
            shape((passages, WIDTH), BF16),
            pltpu.HBM((ROWS, WIDTH), BF16),
            pltpu.HBM((ROWS, 1), F32),
        ),
        [SMEM] + [VMEM] * 2 + [HBM] * 4,
        (VMEM,) * 8 + (HBM,) * 2,
        [
            pltpu.VMEM((queries, WIDTH), F32),
            pltpu.SemaphoreType.DMA((6,)),
        ],
        SCORE, 2_000_000_000, 8_000_000,
        place, tiles, weight, *in_hbm(emb_own, emb_sib, own, sib),
    )


def grad_kernel(
    place, recv, pos_row, exponent, q_r, r_own, r_sib, q_emb, p_emb, q_rows, passages,
    losses, g0, g1, g2, g3, p_grad_own, p_grad_sib, backs_here, w_there,
    dscore, q_grad, p_grad, backs,
):
    x, c = place[0], place[1]
    queries = X * ROWS
    total = recv[0] + recv[1] + recv[2] + recv[3]
    mine = jnp.zeros((1, ROWS), F32)
    for k in range(X):
        mine = mine + jnp.where(x == k, total[k : k + 1], 0.0)
    losses[...] = jnp.log(mine) - total[X : X + 1]
    inverse = 1.0 / flat(total)
    pos = pos_row[...]
    line = lax.broadcasted_iota(jnp.int32, (ROWS, queries), 0)
    for b in range(CHIP_BLOCKS):
        block = pl.ds(b * ROWS, ROWS)
        target = jnp.where(line == pos - b * ROWS, 1.0, 0.0)
        dscore[block, :] = (exponent[block, :] * inverse - target).astype(BF16)

    def keep(rows, emb, r, grad):
        value = back_of(emb, r * score_scale, grad).astype(BF16)
        low, high = value[:, :HALF], value[:, HALF:]
        backs[0, rows, :] = jnp.where(c == 0, low, high)
        backs[1, rows, :] = jnp.where(c == 0, high, low)

    for j in range(WIDTH // HALF):
        cols = pl.ds(j * HALF, HALF)
        q_grad[:, cols] = matmul_tn(dscore[...], p_emb[:, cols])
    for j in range(WIDTH // HALF):
        cols = pl.ds(j * HALF, HALF)
        p_grad[:, cols] = matmul(dscore[...], q_emb[:, cols])
    for k in range(X):
        rows = pl.ds(k * ROWS, ROWS)
        keep(rows, q_emb[rows, :], q_r[rows, :], q_grad[rows, :])
    for k, out in enumerate((g0, g1, g2, g3)):
        rows = pl.ds(pl.multiple_of(lax.rem(x + k, X) * ROWS, ROWS), ROWS)
        out[...] = q_grad[rows, :].astype(out.dtype)
    for b in range(CHIP_BLOCKS):
        rows = pl.ds(b * ROWS, ROWS)
        first = b < BLOCKS
        near = pl.ds((b % BLOCKS) * ROWS, ROWS)
        grad = p_grad[rows, :]
        (p_grad_own if first else p_grad_sib)[near, :] = grad.astype(BF16)
        r = (r_own if first else r_sib)[near, :]
        keep(pl.ds(queries + b * ROWS, ROWS), p_emb[rows, :], r, grad)
    weight_terms(q_rows, passages, backs.at[1], w_there)
    backs_here[...] = backs[0]


def weight_terms(q_rows, passages, backs, out):
    for j in range(WIDTH // HALF):
        cols = pl.ds(j * HALF, HALF)
        hidden = jnp.concatenate([q_rows[:, cols], passages[:, cols]], axis=0)
        out[cols, :] = matmul_tn(hidden, backs[...]).astype(out.dtype)


def grad_side(*args):
    queries = X * ROWS
    passages = CHIP_BLOCKS * ROWS
    tile = shape((ROWS, WIDTH), BF16)
    return call(
        grad_kernel, "grad_side",
        (
            shape((1, ROWS), F32),
            tile, tile, tile, tile,
            shape((OWN, WIDTH), BF16),
            shape((OWN, WIDTH), BF16),
            shape((queries + passages, HALF), BF16),
            shape((WIDTH, HALF), BF16),
        ),
        [SMEM] + [VMEM] * 10,
        (VMEM,) * 9,
        [
            pltpu.VMEM((passages, queries), BF16),
            pltpu.VMEM((queries, WIDTH), F32),
            pltpu.VMEM((passages, WIDTH), F32),
            pltpu.VMEM((C, queries + passages, HALF), BF16),
        ],
        GRAD, 3_000_000_000, 14_000_000,
        *args,
    )


def weight_kernel(backs, q_rows, passages, out):
    weight_terms(q_rows, passages, backs, out)


def weight_here(backs, q_rows, passages):
    return call(
        weight_kernel, "weight_here",
        shape((WIDTH, HALF), F32),
        [VMEM] * 3,
        VMEM,
        [],
        24, 1_350_000_000, 6_000_000,
        backs, q_rows, passages,
    )


def spread_kernel(here, there, out, held, sems):
    own_rows = WIDTH // (Z * Y)
    lanes = HALF // X
    copies = []
    for y in range(Y):
        for h in range(2):
            for z in range(h * Z // 2, (h + 1) * Z // 2):
                rows = pl.ds((z * Y + y) * own_rows, own_rows)
                value = (here[rows, :] + there[rows, :].astype(F32)).astype(BF16)
                for x in range(X):
                    held[y * X + x, z] = value[:, x * lanes : (x + 1) * lanes]
            part = (pl.ds(y * X, X), pl.ds(h * Z // 2, Z // 2))
            copies.append(pltpu.make_async_copy(held.at[part], out.at[part], sems.at[2 * y + h]))
            copies[-1].start()
    for copy in copies:
        copy.wait()


def spread(here, there):
    dims = (Y * X, Z, WIDTH // (Z * Y), HALF // X)
    return call(
        spread_kernel, "spread",
        pltpu.HBM(dims, BF16),
        [VMEM, VMEM],
        HBM,
        [pltpu.VMEM(dims, BF16), pltpu.SemaphoreType.DMA((2 * Y,))],
        16, 500_000, 4_000_000,
        here, there,
    )


def sum_kernel(pieces, out):
    total = pieces[0].astype(F32)
    for k in range(1, pieces.shape[0]):
        total = total + pieces[k].astype(F32)
    out[...] = total.astype(BF16)


def sum_pieces(pieces):
    return call(
        sum_kernel, "sum_pieces", shape(pieces.shape[1:], BF16), [VMEM], VMEM, [], 8, 500_000, 1_000_000, pieces
    )


def last_sum_kernel(pieces, out):
    total = pieces[0].astype(F32)
    for k in range(1, Z):
        total = total + pieces[k].astype(F32)
    total = total * (1.0 / (Z * Y * X * C))
    for d in range(X * C):
        out[d] = total


def last_sum(pieces):
    dims = (X * C,) + pieces.shape[1:]
    return call(
        last_sum_kernel, "last_sum", shape(dims, F32), [VMEM], VMEM, [], 8, 50_000, 100_000, pieces
    )


def lay_kernel(pieces, out):
    lanes = HALF // X
    for x in range(X):
        for c in range(C):
            out[:, c * HALF + x * lanes : c * HALF + (x + 1) * lanes] = pieces[x * C + c]


def lay(pieces):
    dims = (WIDTH // (Z * Y), WIDTH)
    return call(lay_kernel, "lay", shape(dims, F32), [VMEM], VMEM, [], 8, 0, 200_000, pieces)


def hidden_kernel(*refs):
    *terms, emb, r, weight, out = refs
    grad = terms[0][...].astype(F32)
    for term in terms[1:]:
        grad = grad + term[...].astype(F32)
    back = back_of(emb[...], r[...] * score_scale, grad).astype(BF16)
    for j in range(WIDTH // PART):
        cols = pl.ds(j * PART, PART)
        out[:, cols] = matmul_nt(back, weight[cols, :]).astype(BF16)


def hidden_grad(terms, emb, r, weight, far=False):
    rows = emb.shape[0]
    return call(
        hidden_kernel, "hidden_grad",
        shape((rows, WIDTH), BF16),
        [VMEM] * (len(terms) + 3),
        VMEM,
        [],
        24, 2 * rows * WIDTH * WIDTH, 2_000_000 + rows * 10_000,
        *(in_hbm(terms[0]) if far else terms[:1]), *terms[1:], *in_hbm(emb, r), weight,
    )


def body(queries, passages, weight, pairs, positive):
    x = lax.axis_index("x")
    c = lax.axis_index("c")
    place = jnp.stack([x, c]).astype(jnp.int32)

    packed = pack(queries, positive, pairs)
    tiles = exchange(packed, "x")
    passages, weight, _ = lax.optimization_barrier((passages, weight, packed))
    emb_own, r_own = passage_side(passages, weight)
    outgoing, _ = lax.optimization_barrier((passages, emb_own))
    sibling = lax.ppermute(outgoing, "c", SWAP)
    emb_sib, r_sib = passage_side(sibling, weight)

    q_emb, q_r, exponent, send, pos_row, p_emb, q_rows, hidden, emb_mine, r_mine = score_side(
        place, tiles, weight, emb_own, emb_sib, passages, sibling
    )
    recv = exchange(send, "x")
    losses, g0, g1, g2, g3, p_grad, p_grad_sib, backs, w_there = grad_side(
        place, recv, pos_row, exponent, q_r, r_own, r_sib, q_emb, p_emb, q_rows, hidden
    )

    w_there = lax.ppermute(w_there, "c", SWAP)
    w = spread(weight_here(backs, q_rows, hidden), w_there)
    (p_grad_sib, g1, g2, g3), w = lax.optimization_barrier(((p_grad_sib, g1, g2, g3), w))
    g2 = lax.ppermute(g2, "x", shift(X - 2))
    g1 = lax.ppermute(g1, "x", shift(X - 1))
    g3 = lax.ppermute(g3, "x", shift(X - 3))
    query_grad = hidden_grad((g0, g1, g2, g3), emb_mine, r_mine, weight)
    p_grad_sib = lax.ppermute(p_grad_sib, "c", SWAP)
    passage_grad = hidden_grad((p_grad, p_grad_sib), emb_own, r_own, weight, far=True)

    w = sum_pieces(exchange(w, ("y", "x")))
    w, passage_grad = lax.optimization_barrier((w, passage_grad))
    w = exchange(w, "z")
    w, query_grad = lax.optimization_barrier((w, query_grad))
    w = last_sum(w)
    weight_grad = lay(exchange(w, ("x", "c")))
    return losses.reshape(ROWS), query_grad, passage_grad, weight_grad


def solution(mesh):
    torus = Mesh(mesh.devices.reshape(Z, Y, X, C), ("z", "y", "x", "c"))
    every = ("z", "y", "x", "c")
    return jax.shard_map(
        body,
        mesh=torus,
        in_specs=(P(every, None), P(every, None), P(), P(every, None), P(every)),
        out_specs=(P(every), P(every, None), P(every, None), P(("z", "y"), None)),
        check_vma=False,
    )
```
